32 devices in a mesh: rows: 8 (over z, y), seq: 4 (over x, core).
Axes of the slice: x: 2, y: 2, z: 4, core: 2. Of those that a mesh axis runs over, the one named last changes fastest.
Arguments:
- inputs: bfloat16 [32, 1024, 1280], P('rows', 'seq'), may hold values from -6 to 6
- segment_ids: int32 [32, 1024], P('rows', 'seq'), may hold values from 0 to 3, as said below
- cotangent: bfloat16 [32, 1024, 1280], P('rows', 'seq'), may hold values from -6 to 6
- norm1_gain: float32 [1280], replicated, may hold values from 0.25 to 1.75
- norm1_shift: float32 [1280], replicated, may hold values from -3 to 3
- down_weight: bfloat16 [1280, 640], replicated, may hold values from -0.15625 to 0.15625
- down_bias: float32 [640], replicated, may hold values from -3 to 3
- norm2_gain: float32 [640], replicated, may hold values from 0.25 to 1.75
- norm2_shift: float32 [640], replicated, may hold values from -3 to 3
- conv_weight: bfloat16 [5, 640, 640], replicated, may hold values from -0.15625 to 0.15625
- conv_bias: float32 [640], replicated, may hold values from -3 to 3
- norm3_gain: float32 [640], replicated, may hold values from 0.25 to 1.75
- norm3_shift: float32 [640], replicated, may hold values from -3 to 3
- up_weight: bfloat16 [640, 1280], replicated, may hold values from -0.3125 to 0.3125
- up_bias: float32 [1280], replicated, may hold values from -3 to 3
Outputs:
- output: bfloat16 [32, 1024, 1280], P('rows', 'seq')
- input_grad: bfloat16 [32, 1024, 1280], P('rows', 'seq')
- norm1_gain_grad: float32 [1280], replicated
- norm1_shift_grad: float32 [1280], replicated
- down_weight_grad: float32 [1280, 640], P('rows', 'seq')
- down_bias_grad: float32 [640], replicated
- norm2_gain_grad: float32 [640], replicated
- norm2_shift_grad: float32 [640], replicated
- conv_weight_grad: float32 [5, 640, 640], P(None, 'rows', 'seq')
- conv_bias_grad: float32 [640], replicated
- norm3_gain_grad: float32 [640], replicated
- norm3_shift_grad: float32 [640], replicated
- up_weight_grad: float32 [640, 1280], P('rows', 'seq')
- up_bias_grad: float32 [1280], replicated
The draws below stay inside these ranges and needn't reach their ends.
Inputs may be any that keep to these rules, and one draw needn't show every extreme that they name: `segment_ids`: within each row the ids never fall and begin at 0; a new id starts a new protein. Of the 4 rows held by one index of rows, one row drawn from the seed is a single protein; every other row holds exactly 4 proteins, whose bounds are drawn from the seed.
All inputs are finite; a program needn't handle non-finite values.
Results may differ from the reference program's by a relative error of at most 0.015.
Values may be sent and summed in bfloat16 or wider, within the bound.
A program may use at most 192 MiB of HBM per device.

```python
import jax
import jax.numpy as jnp
from jax import lax

D = 1280
HID = 640
TAPS = 5
DILATION = 128
MICRO = 4
LEN_DEV = 256
LEN = 1024
ROWS = 32


def draw_segment_ids(key, part):
    key = jax.random.fold_in(key, 11)
    key_starts, key_single = jax.random.split(key)
    row_keys = jax.random.split(key_starts, ROWS)
    proteins = LEN // LEN_DEV

    def row_starts(row_key):
        order = jax.random.permutation(row_key, LEN - 1)
        picked = order[:proteins - 1] + 1
        return jnp.zeros((LEN,), jnp.int32).at[picked].set(1)
    starts = jax.vmap(row_starts)(row_keys)
    chosen = jax.random.randint(key_single, (ROWS // MICRO,), 0, MICRO)
    local_index = jnp.arange(ROWS, dtype=jnp.int32) % MICRO
    single = local_index == jnp.repeat(chosen, MICRO)
    starts = starts * (1 - single.astype(jnp.int32))[:, None]
    return jnp.cumsum(starts, axis=1).astype(jnp.int32)


def levels(rng, dims, pieces, least, high):
    level, own = 1.0, jax.random.fold_in(rng, 6)
    for position, blocks in pieces:
        heights = jnp.exp(jax.random.uniform(jax.random.fold_in(own, position), (blocks,), jnp.float32, least / len(pieces), high / len(pieces)))
        level = level * jnp.repeat(heights, dims[position] // blocks).reshape([-1 if axis == position else 1 for axis in range(len(dims))])
    return level


def normal_values(rng, shape, spread, bound, shards=(), kind=jnp.bfloat16):
    values = spread * jax.random.normal(rng, shape, jnp.float32)
    if shards:
        values = values * levels(rng, shape, shards, -0.22, 0.18)
    return jnp.clip(values, -bound, bound).astype(kind)


def setup_inputs(seed: int = 0) -> dict:
    streams_of = jax.random.split(jax.random.key(seed), 16)
    inputs = normal_values(streams_of[0], (ROWS, LEN, D), 1.0, 6.0, ((0, 8), (1, 4)))
    segment_ids = draw_segment_ids(jax.random.fold_in(streams_of[15], 71), 0)
    cotangent = normal_values(streams_of[2], (ROWS, LEN, D), 1.0, 6.0, ((0, 8), (1, 4)))
    norm1_gain = jnp.clip(1.0 + 0.15 * jax.random.normal(streams_of[3], (D,), jnp.float32), 0.25, 1.75)
    norm1_shift = normal_values(streams_of[4], (D,), 0.5, 3.0, (), jnp.float32)
    down_weight = normal_values(streams_of[5], (D, HID), D ** -0.5, 0.15625)
    down_bias = normal_values(streams_of[6], (HID,), 0.5, 3.0, (), jnp.float32)
    norm2_gain = jnp.clip(1.0 + 0.15 * jax.random.normal(streams_of[7], (HID,), jnp.float32), 0.25, 1.75)
    norm2_shift = normal_values(streams_of[8], (HID,), 0.5, 3.0, (), jnp.float32)
    conv_weight = normal_values(streams_of[9], (TAPS, HID, HID), (TAPS * HID // 2) ** -0.5, 0.15625)
    conv_bias = normal_values(streams_of[10], (HID,), 0.5, 3.0, (), jnp.float32)
    norm3_gain = jnp.clip(1.0 + 0.15 * jax.random.normal(streams_of[11], (HID,), jnp.float32), 0.25, 1.75)
    norm3_shift = normal_values(streams_of[12], (HID,), 0.5, 3.0, (), jnp.float32)
    up_weight = normal_values(streams_of[13], (HID, D), (HID // 2) ** -0.5, 0.3125)
    up_bias = normal_values(streams_of[14], (D,), 0.5, 3.0, (), jnp.float32)
    return {"inputs": inputs, "segment_ids": segment_ids, "cotangent": cotangent, "norm1_gain": norm1_gain, "norm1_shift": norm1_shift, "down_weight": down_weight, "down_bias": down_bias, "norm2_gain": norm2_gain, "norm2_shift": norm2_shift, "conv_weight": conv_weight, "conv_bias": conv_bias, "norm3_gain": norm3_gain, "norm3_shift": norm3_shift, "up_weight": up_weight, "up_bias": up_bias}


@jax.custom_vjp
def low(v):
    return lax.optimization_barrier(v.astype(jnp.bfloat16)).astype(jnp.float32)

@jax.custom_vjp
def low_back(v):
    return v

def low_keep(v):
    return (low(v), None)

def low_pass(kept, grad):
    return (grad,)

def back_keep(v):
    return (v, None)

def back_low(kept, grad):
    return (low(grad),)
low.defvjp(low_keep, low_pass)
low_back.defvjp(back_keep, back_low)
EPSILON = 1e-05
HIGHEST = lax.Precision.HIGHEST

def layer_norm(values, gain, shift):
    centred = values - lax.optimization_barrier(jnp.mean(values, axis=-1, keepdims=True))
    second_moment = lax.optimization_barrier(jnp.mean(centred * centred, axis=-1, keepdims=True))
    return centred * lax.rsqrt(second_moment + EPSILON) * gain + shift

def smooth(values):
    return jax.nn.gelu(values, approximate=False)

def dilated(hidden, labels, weights):
    length = hidden.shape[0]
    margin = TAPS // 2 * DILATION
    padded = jnp.pad(hidden, ((margin, margin), (0, 0)))
    labelled = jnp.pad(labels + 1, (margin, margin))
    centre = labelled[margin:margin + length]
    total = jnp.zeros((length, weights.shape[2]), jnp.float32)
    for tap_index in range(TAPS):
        offset = tap_index * DILATION
        keeping = (labelled[offset:offset + length] == centre).astype(jnp.float32)
        total = total + jnp.dot(padded[offset:offset + length] * keeping[:, None], weights[tap_index], precision=HIGHEST)
    return total

def row_block(values, labels, norm1_gain, norm1_shift, down_weight, down_bias, norm2_gain, norm2_shift, conv_weight, conv_bias, norm3_gain, norm3_shift, up_weight, up_bias):
    first = low(smooth(layer_norm(values, norm1_gain, norm1_shift)))
    reduced = low_back(jnp.dot(first, down_weight, precision=HIGHEST) + down_bias)
    second = low(low_back(smooth(layer_norm(reduced, norm2_gain, norm2_shift))))
    mixed = low_back(low(dilated(second, labels, conv_weight) + conv_bias))
    third = low(smooth(layer_norm(mixed, norm3_gain, norm3_shift)))
    return values + jnp.dot(third, up_weight, precision=HIGHEST) + up_bias

def reference(inputs, segment_ids, cotangent, norm1_gain, norm1_shift, down_weight, down_bias, norm2_gain, norm2_shift, conv_weight, conv_bias, norm3_gain, norm3_shift, up_weight, up_bias):
    params = tuple((item.astype(jnp.float32) for item in (norm1_gain, norm1_shift, down_weight, down_bias, norm2_gain, norm2_shift, conv_weight, conv_bias, norm3_gain, norm3_shift, up_weight, up_bias)))

    def per_row(totals, sliced):
        values, labels, incoming = sliced

        def forward(inputs_row, *weights):
            return row_block(inputs_row, labels, *weights)
        result, pullback = jax.vjp(forward, values.astype(jnp.float32), *params)
        grads = pullback(incoming.astype(jnp.float32))
        totals = tuple((left + right for left, right in zip(totals, grads[1:])))
        return (totals, (result.astype(jnp.bfloat16), grads[0].astype(jnp.bfloat16)))
    initial = tuple((jnp.zeros_like(item) for item in params))
    totals, stacked = lax.scan(per_row, initial, (inputs, segment_ids, cotangent))
    return (stacked[0], stacked[1], totals[0], totals[1], totals[2], totals[3], totals[4], totals[5], totals[6], totals[7], totals[8], totals[9], totals[10], totals[11])
```

```python
import functools
import math

import jax
import jax.numpy as jnp
from jax import lax
from jax.experimental import pallas as pl
from jax.experimental.pallas import tpu as pltpu
from jax.sharding import PartitionSpec as P

DILATION = 128
EPSILON = 1e-05
MESH = pl.DeviceIdType.MESH
bf16 = jnp.bfloat16
f32 = jnp.float32
ANY = pl.BlockSpec(memory_space=pl.ANY)
VMEM = pl.BlockSpec(memory_space=pltpu.VMEM)


def up_to(value, step):
    return -(-value // step) * step


def normalise(values):
    mean = jnp.mean(values, axis=-1, keepdims=True)
    centred = values - mean
    scale = lax.rsqrt(jnp.mean(centred * centred, axis=-1, keepdims=True) + EPSILON)
    return mean, scale, centred * scale


def gelu_and_slope(values):
    phi = 0.5 + 0.5 * lax.erf(values * math.sqrt(0.5))
    density = jnp.exp(-0.5 * values * values) * (1.0 / math.sqrt(2.0 * math.pi))
    return values * phi, phi + values * density


def norm_back(grad, normal, scale):
    mean = jnp.mean(grad, axis=-1, keepdims=True)
    along = jnp.mean(grad * normal, axis=-1, keepdims=True)
    return scale * (grad - mean - normal * along)


def fold(values):
    rows, width = values.shape
    return jnp.sum(values.reshape(rows // 8, 8, width), axis=0)


def dot(left, right):
    return jnp.dot(left, right, preferred_element_type=f32)


def dot_rows(left, right):
    return lax.dot_general(left, right, (((0,), (0,)), ((), ())), preferred_element_type=f32)


def dot_cols(left, right):
    return lax.dot_general(left, right, (((1,), (1,)), ((), ())), preferred_element_type=f32)


class Place:
    def __init__(self, rows, seq):
        self.rows, self.seq = rows, seq
        self.r, self.s = lax.axis_index("rows"), lax.axis_index("seq")
        self.size = {"c": 2, "x": seq // 2, "y": 2, "z": rows // 2}
        self.at = {
            "c": lax.rem(self.s, 2),
            "x": lax.div(self.s, 2),
            "y": lax.rem(self.r, 2),
            "z": lax.div(self.r, 2),
        }

    def peer(self, dim, index):
        at = dict(self.at)
        at[dim] = index
        return (at["z"] * 2 + at["y"], at["x"] * 2 + at["c"])


def split(index):
    return lax.div(index, 2), lax.rem(index, 2)


class Reduction:
    def __init__(self, place, order, send, got, send_sem, recv_sem):
        self.place, self.order = place, ("c",) + order
        self.send, self.got, self.send_sem, self.recv_sem = send, got, send_sem, recv_sem
        self.at = [place.at[d] for d in self.order]
        self.size = [place.size[d] for d in self.order]

    def index(self, r, s):
        z, y = split(r)
        where = {"c": s % 2, "x": s // 2, "y": y, "z": z}
        return tuple(where[d] for d in self.order)

    def copies(self, stage):
        n, at = self.size[stage], self.at[stage]
        found = []
        for off in range(1, n):
            other = lax.rem(at + off, n)
            slot = n - 1 - off
            found.append(
                (
                    other,
                    functools.partial(
                        pltpu.make_async_remote_copy,
                        src_ref=self.send.at[tuple(self.at[:stage]) + (other,)],
                        dst_ref=self.got[stage].at[slot],
                        send_sem=self.send_sem.at[stage, slot],
                        recv_sem=self.recv_sem.at[stage, slot],
                        device_id=self.place.peer(self.order[stage], other),
                        device_id_type=MESH,
                    ),
                )
            )
        return found

    def total(self, stage, prefix, rest):
        value = self.send[tuple(prefix) + rest].astype(f32)
        for s in range(stage):
            for slot in range(self.size[s] - 1):
                value = value + self.got[s][(slot,) + tuple(prefix[s + 1 :]) + rest].astype(f32)
        return value

    def start(self):
        for _, copy in self.copies(0):
            copy().start()

    def step(self, stage):
        for _, copy in self.copies(stage - 1):
            copy().wait_recv()
        for other, copy in self.copies(stage):
            prefix = self.at[:stage] + [other]
            lead = self.size[stage + 1 :]
            if not lead:
                self.send[tuple(prefix)] = self.total(stage, prefix, ()).astype(bf16)
            else:
                count = math.prod(lead)

                def add(i, carry, prefix=prefix, lead=lead):
                    rest = []
                    for n in reversed(lead):
                        rest.insert(0, lax.rem(i, n))
                        i = lax.div(i, n)
                    rest = tuple(rest)
                    self.send[tuple(prefix) + rest] = self.total(stage, prefix, rest).astype(bf16)
                    return carry

                lax.fori_loop(0, count, add, 0)
            copy().start()

    def finish(self):
        for _, copy in self.copies(3):
            copy().wait_recv()
        return self.total(4, self.at, ())

    def drain(self):
        for stage in range(4):
            for _, copy in self.copies(stage):
                copy().wait_send()


ORDERS = {"up": ("y", "x", "z"), "conv": ("y", "x", "z"), "last": ("x", "y", "z"), "down": ("x", "y", "z")}
JOBS = ("up", "conv", "last", "down")


class Sizes:
    def __init__(self, rows, seq, micro, length, width, inner, taps):
        self.rows, self.seq = rows, seq
        self.micro, self.length, self.width, self.inner, self.taps = micro, length, width, inner, taps
        self.positions = micro * length
        self.margin = taps // 2 * DILATION
        assert self.margin <= length
        self.up = (inner // rows, width // seq)
        self.conv = (inner // rows, inner // seq)
        self.down = (width // rows, inner // seq)
        self.tap_width = up_to(self.conv[0], 16) // 16 * self.conv[1]
        assert width == 2 * inner and micro % 2 == 0 and micro // 2 * length <= inner

    def packed(self, share):
        groups = up_to(share[0], 16) // 16
        return (16, up_to(groups * share[1], 128))

    def blocks(self):
        return {
            "up": self.packed(self.up),
            "conv": (16, up_to((self.taps - 1) * self.tap_width, 128)),
            "last": self.packed(self.conv),
            "down": self.packed(self.down),
        }


def pack(piece, width):
    rows, columns = piece.shape
    padded = up_to(rows, 16)
    if padded > rows:
        piece = jnp.concatenate([piece, jnp.zeros((padded - rows, columns), f32)], axis=0)
    parts = [piece[k : k + 16] for k in range(0, padded, 16)]
    rest = width - len(parts) * columns
    if rest:
        parts.append(jnp.zeros((16, rest), f32))
    return jnp.concatenate(parts, axis=1).astype(bf16)


def unpack(value, ref, share):
    rows, columns = share
    for k in range(0, rows, 16):
        count = min(16, rows - k)
        begin = k // 16 * columns
        ref[k : k + count, :] = value[:count, begin : begin + columns]


def kernel(sizes, *refs):
    (
        x_hbm, seg, c_hbm, n1g, n1s, wd_hbm, db, n2g, n2s, wc_hbm, cb, n3g, n3s, wu_hbm, ub,
        out_hbm, ig_hbm, vec_out, down_out, conv_out, up_out,
        x, c, wd, wc, wu, first, slope1, stat1, normal2, scale2, slope2, sext, gext, masks,
        third, rg, staged, product, own_labels, labels,
        sum1, sum2, vec_own, vec_part, vec_got, vec_far,
        load_sem, store_sem, halo_send, halo_recv, label_send, label_recv, vec_send, vec_recv,
        *job_refs,
    ) = refs
    z = sizes
    micro, length, width, inner, taps = z.micro, z.length, z.width, z.inner, z.taps
    place = Place(z.rows, z.seq)
    me_r, me_s = place.r, place.s
    has_left, has_right = me_s > 0, me_s < z.seq - 1
    left = (me_r, jnp.maximum(me_s - 1, 0))
    right = (me_r, jnp.minimum(me_s + 1, z.seq - 1))
    masked = rg
    jobs = {}
    for number, name in enumerate(JOBS):
        send, g0, g1, g2, g3, ss, rs = job_refs[7 * number : 7 * number + 7]
        jobs[name] = Reduction(place, ORDERS[name], send, (g0, g1, g2, g3), ss, rs)

    def load_rows(source, target, base, i):
        return pltpu.make_async_copy(source.at[i], target.at[i], load_sem.at[base + i])

    weight_loads = [
        pltpu.make_async_copy(source, target, load_sem.at[2 * micro + k])
        for k, (source, target) in enumerate(((wd_hbm, wd), (wu_hbm, wu), (wc_hbm, wc)))
    ]
    load_rows(x_hbm, x, 0, 0).start()
    weight_loads[0].start()
    for i in range(1, micro):
        load_rows(x_hbm, x, 0, i).start()
    for i in range(micro):
        load_rows(c_hbm, c, micro, i).start()
    weight_loads[1].start()
    weight_loads[2].start()

    barrier = pltpu.get_barrier_semaphore()
    for off in range(1, z.seq):
        pl.semaphore_signal(
            barrier, inc=1, device_id=(me_r, lax.rem(me_s + off, z.seq)), device_id_type=MESH
        )
    for off in range(1, z.rows):
        pl.semaphore_signal(
            barrier, inc=1, device_id=(lax.rem(me_r + off, z.rows), me_s), device_id_type=MESH
        )

    own_labels[...] = jnp.zeros(own_labels.shape, jnp.int32)
    own_labels[0:micro, :] = seg[...]
    sum1[...] = jnp.zeros(sum1.shape, f32)
    sum2[...] = jnp.zeros(sum2.shape, f32)
    vec_own[...] = jnp.zeros(vec_own.shape, f32)

    @pl.when(jnp.logical_not(has_left))
    def _():
        labels[0] = jnp.full(labels.shape[1:], -1, jnp.int32)
        sext[:, 0:length, :] = jnp.zeros((micro, length, inner), bf16)
        gext[:, 0:length, :] = jnp.zeros((micro, length, inner), bf16)

    @pl.when(jnp.logical_not(has_right))
    def _():
        labels[1] = jnp.full(labels.shape[1:], -1, jnp.int32)
        sext[:, 2 * length :, :] = jnp.zeros((micro, length, inner), bf16)
        gext[:, 2 * length :, :] = jnp.zeros((micro, length, inner), bf16)

    def halo(ext, turn, i):
        return (
            (
                has_right,
                pltpu.make_async_remote_copy(
                    src_ref=ext.at[i, pl.ds(length, length)],
                    dst_ref=ext.at[i, pl.ds(0, length)],
                    send_sem=halo_send.at[turn, 0, i],
                    recv_sem=halo_recv.at[turn, 0, i],
                    device_id=right,
                    device_id_type=MESH,
                ),
            ),
            (
                has_left,
                pltpu.make_async_remote_copy(
                    src_ref=ext.at[i, pl.ds(length, length)],
                    dst_ref=ext.at[i, pl.ds(2 * length, length)],
                    send_sem=halo_send.at[turn, 1, i],
                    recv_sem=halo_recv.at[turn, 1, i],
                    device_id=left,
                    device_id_type=MESH,
                ),
            ),
        )

    def label_copies():
        return [
            (
                ok,
                pltpu.make_async_remote_copy(
                    src_ref=own_labels,
                    dst_ref=labels.at[way],
                    send_sem=label_send.at[way],
                    recv_sem=label_recv.at[way],
                    device_id=target,
                    device_id_type=MESH,
                ),
            )
            for way, (ok, target) in enumerate(((has_right, right), (has_left, left)))
        ]

    def start_all(copies):
        for ok, copy in copies:
            pl.when(ok)(copy.start)

    def wait_sent(copies):
        for ok, copy in copies:
            pl.when(ok)(copy.wait_send)

    def wait_got(copies):
        pl.when(has_left)(copies[0][1].wait_recv)
        pl.when(has_right)(copies[1][1].wait_recv)

    def first_half(i):
        load_rows(x_hbm, x, 0, i).wait()
        chunk = min(128, length)
        for begin in range(0, length, chunk):
            some = pl.ds(begin, chunk)
            mean, scale, normal = normalise(x[i, some, :].astype(f32))
            act, slope = gelu_and_slope(normal * n1g[...] + n1s[...])
            first[i, some, :] = act.astype(bf16)
            slope1[i, some, :] = slope.astype(bf16)
            stat1[0, i, some, :] = jnp.broadcast_to(mean, (chunk, 128))
            stat1[1, i, some, :] = jnp.broadcast_to(scale, (chunk, 128))

    def second_half(i):
        reduced = dot(first[i], wd[...]) + db[...]
        _, scale, normal = normalise(reduced)
        act, slope = gelu_and_slope(normal * n2g[...] + n2s[...])
        sext[i, pl.ds(length, length), :] = act.astype(bf16)
        slope2[i] = slope.astype(bf16)
        normal2[i] = normal.astype(bf16)
        scale2[i] = jnp.broadcast_to(scale, (length, 128))

    first_half(0)
    weight_loads[0].wait()
    second_half(0)
    pl.semaphore_wait(barrier, z.seq + z.rows - 2)
    start_all(label_copies())
    start_all(halo(sext, 0, 0))

    def head(i, carry):
        first_half(i)
        second_half(i)
        start_all(halo(sext, 0, i))
        return carry

    lax.fori_loop(1, micro, head, 0)

    def third_grad_at(i):
        row, column = split(i)
        return (
            pl.ds(pl.multiple_of(row * length, 128), length),
            pl.ds(pl.multiple_of(column * inner, 128), inner),
        )

    weight_loads[1].wait()

    def third_back(i, carry):
        load_rows(c_hbm, c, micro, i).wait()
        product[third_grad_at(i)] = dot_cols(c[i], wu[...])
        sum1[0] += fold(c[i].astype(f32))
        return carry

    lax.fori_loop(0, micro, third_back, 0)

    wait_got(label_copies())
    spread = jnp.concatenate([labels[0], own_labels[...], labels[1]], axis=1).astype(f32).T
    for i in range(micro):
        column = spread[:, i : i + 1]
        centre = column[length : 2 * length]
        for k in range(taps):
            begin = length - z.margin + k * DILATION
            same = (column[begin : begin + length] == centre).astype(f32)
            masks[k, i] = jnp.broadcast_to(same, (length, 128)).astype(bf16)

    def tap_of(ext, i, k):
        begin = length - z.margin + k * DILATION
        block = ext[i, pl.ds(begin, length), :]
        if k == taps // 2:
            return block
        keep = masks[k, i]
        return block * jnp.concatenate([keep] * (inner // 128), axis=1)

    weight_loads[2].wait()

    def middle(i):
        wait_got(halo(sext, 0, i))
        conv = dot(tap_of(sext, i, 0), wc[0])
        for k in range(1, taps):
            conv = conv + dot(tap_of(sext, i, k), wc[k])
        mixed = (conv + cb[...]).astype(bf16).astype(f32)
        _, scale, normal = normalise(mixed)
        act, slope = gelu_and_slope(normal * n3g[...] + n3s[...])
        third[i] = act.astype(bf16)
        grad = product[third_grad_at(i)] * slope
        sum2[0] += fold(grad * normal)
        sum2[1] += fold(grad)
        mixed_grad = norm_back(grad * n3g[...], normal, scale).astype(bf16)
        gext[i, pl.ds(length, length), :] = mixed_grad
        sum2[2] += fold(mixed_grad.astype(f32))

    def middle_step(i, carry):
        middle(i)
        return carry

    lax.fori_loop(0, micro - 1, middle_step, 0)
    for i in range(micro):
        wait_sent(halo(sext, 0, i))
    for i in range(micro - 1):
        start_all(halo(gext, 1, i))
    middle(micro - 1)
    start_all(halo(gext, 1, micro - 1))

    whole = lambda ref: ref[...].reshape(z.positions, ref.shape[-1])
    own = lambda ext: ext[:, length : 2 * length, :].reshape(z.positions, inner)
    product[...] = dot_rows(whole(third), whole(c))
    up_block, conv_block, last_block, down_block = (z.blocks()[name] for name in JOBS)

    def pack_up(r, carry):
        share = z.up
        rows = product[pl.ds(pl.multiple_of(r * share[0], 8), share[0]), :]
        for s in range(z.seq):
            piece = rows[:, s * share[1] : (s + 1) * share[1]]
            jobs["up"].send[jobs["up"].index(r, s)] = pack(piece, up_block[1])
        return carry

    lax.fori_loop(0, z.rows, pack_up, 0)
    jobs["up"].start()

    for k in range(taps):
        if k == taps // 2:
            source = own(sext)
        else:

            def mask_rows(i, carry, k=k):
                masked[i] = tap_of(sext, i, k)
                return carry

            lax.fori_loop(0, micro, mask_rows, 0)
            source = whole(masked)
        product[:, 0:inner] = dot_rows(source, own(gext))

        def pack_tap(r, carry, k=k):
            share = z.conv
            rows = product[pl.ds(pl.multiple_of(r * share[0], 8), share[0]), :]
            for s in range(z.seq):
                piece = rows[:, s * share[1] : (s + 1) * share[1]]
                if k == taps - 1:
                    jobs["last"].send[jobs["last"].index(r, s)] = pack(piece, last_block[1])
                else:
                    at = jobs["conv"].index(r, s)
                    lanes = pl.ds(k * z.tap_width, z.tap_width)
                    jobs["conv"].send[at + (slice(None), lanes)] = pack(piece, z.tap_width)
            return carry

        lax.fori_loop(0, z.rows, pack_tap, 0)
        if k == 0:
            jobs["up"].step(1)
        if k == taps - 2:
            jobs["conv"].start()
    jobs["last"].start()
    jobs["conv"].step(1)
    jobs["last"].step(1)

    def store_rows(source, target, base, i):
        return pltpu.make_async_copy(source.at[i], target.at[i], store_sem.at[base + i])

    def finish_output(i, carry):
        result = x[i].astype(f32) + dot(third[i], wu[...]) + ub[...]
        staged[i] = result.astype(bf16)
        store_rows(staged, out_hbm, 0, i).start()
        return carry

    lax.fori_loop(0, micro, finish_output, 0)

    def conv_back(i, carry):
        wait_got(halo(gext, 1, i))
        grad = dot_cols(tap_of(gext, i, 0), wc[taps - 1])
        for k in range(1, taps):
            grad = grad + dot_cols(tap_of(gext, i, k), wc[taps - 1 - k])
        grad = grad.astype(bf16).astype(f32) * slope2[i].astype(f32)
        normal = normal2[i].astype(f32)
        sum2[3] += fold(grad * normal)
        sum2[4] += fold(grad)
        scale = jnp.concatenate([scale2[i]] * (inner // 128), axis=1)
        reduced_grad = norm_back(grad * n2g[...], normal, scale).astype(bf16)
        rg[i] = reduced_grad
        sum2[5] += fold(reduced_grad.astype(f32))
        return carry

    lax.fori_loop(0, micro, conv_back, 0)

    half = width // 2
    for h in range(2):
        side = first[:, :, h * half : (h + 1) * half].reshape(z.positions, half)
        product[:, h * inner : (h + 1) * inner] = dot_rows(side, whole(rg))

    for h in range(2):

        def pack_down(r, carry, h=h):
            share = z.down
            rows = product[pl.ds(pl.multiple_of(r * share[0], 8), share[0]), h * inner : (h + 1) * inner]
            for s in range(z.seq):
                piece = rows[:, s * share[1] : (s + 1) * share[1]]
                at = jobs["down"].index(r + h * (z.rows // 2), s)
                jobs["down"].send[at] = pack(piece, down_block[1])
            return carry

        lax.fori_loop(0, z.rows // 2, pack_down, 0)
    jobs["down"].start()

    def vector_copies(turn, stage):
        count, me = ((z.seq, me_s), (z.rows, me_r))[stage]
        source = (vec_own, vec_part)[stage].at[turn]
        got = (vec_got, vec_far)[stage]
        sends, gets = [], []
        for off in range(1, count):
            other = lax.rem(me + off, count)
            target = ((me_r, other), (other, me_s))[stage]
            for found, slot in ((sends, me), (gets, other)):
                found.append(
                    functools.partial(
                        pltpu.make_async_remote_copy,
                        src_ref=source,
                        dst_ref=got.at[turn, slot],
                        send_sem=vec_send.at[turn, stage, off],
                        recv_sem=vec_recv.at[turn, stage, slot],
                        device_id=target,
                        device_id_type=MESH,
                    )
                )
        return sends, gets

    def vector_start(turn, stage):
        for copy in vector_copies(turn, stage)[0]:
            copy().start()

    def vector_total(turn, stage):
        count, me = ((z.seq, me_s), (z.rows, me_r))[stage]
        for copy in vector_copies(turn, stage)[1]:
            copy().wait_recv()
        source, got = ((vec_own, vec_got), (vec_part, vec_far))[stage]
        got[turn, me] = source[turn]
        total = got[turn, 0]
        for k in range(1, count):
            total = total + got[turn, k]
        return total

    def squeeze(value):
        return jnp.sum(value, axis=0, keepdims=True)

    early = [squeeze(sum1[0, :, h * half : (h + 1) * half]) for h in range(2)]
    early += [squeeze(sum2[k]) for k in range(6)]
    for k, row in enumerate(early):
        vec_own[0, k : k + 1, :] = row
    vector_start(0, 0)

    jobs["up"].step(2)
    jobs["conv"].step(2)
    jobs["last"].step(2)

    def tail(i, carry):
        grads = dot_cols(rg[i], wd[...])
        chunk = min(128, length)
        for begin in range(0, length, chunk):
            some = pl.ds(begin, chunk)
            grad = grads[begin : begin + chunk] * slope1[i, some, :].astype(f32)
            mean = jnp.concatenate([stat1[0, i, some, :]] * (width // 128), axis=1)
            scale = jnp.concatenate([stat1[1, i, some, :]] * (width // 128), axis=1)
            normal = (x[i, some, :].astype(f32) - mean) * scale
            sum1[1] += fold(grad * normal)
            sum1[2] += fold(grad)
            part = norm_back(grad * n1g[...], normal, scale)
            c[i, some, :] = (c[i, some, :].astype(f32) + part).astype(bf16)
        store_rows(c, ig_hbm, micro, i).start()
        return carry

    lax.fori_loop(0, micro, tail, 0)
    late = [squeeze(sum1[k, :, h * half : (h + 1) * half]) for k in (1, 2) for h in range(2)]
    for k, row in enumerate(late):
        vec_own[1, k : k + 1, :] = row
    vector_start(1, 0)
    vec_part[0] = vector_total(0, 0)
    vector_start(0, 1)

    jobs["down"].step(1)
    jobs["up"].step(3)
    vec_part[1] = vector_total(1, 0)
    vector_start(1, 1)
    jobs["conv"].step(3)
    jobs["last"].step(3)
    jobs["down"].step(2)
    jobs["down"].step(3)
    for turn in range(2):
        vec_out[8 * turn : 8 * turn + 8, :] = vector_total(turn, 1)
    unpack(jobs["up"].finish(), up_out, z.up)
    value = jobs["conv"].finish()
    for k in range(taps - 1):
        unpack(value[:, k * z.tap_width : (k + 1) * z.tap_width], conv_out.at[k], z.conv)
    unpack(jobs["last"].finish(), conv_out.at[taps - 1], z.conv)
    unpack(jobs["down"].finish(), down_out, z.down)

    for i in range(micro):
        store_rows(staged, out_hbm, 0, i).wait()
        store_rows(c, ig_hbm, micro, i).wait()
        wait_sent(halo(gext, 1, i))
    wait_sent(label_copies())
    for turn in range(2):
        for stage in range(2):
            for copy in vector_copies(turn, stage)[0]:
                copy().wait_send()
    for job in jobs.values():
        job.drain()


def per_device(z, x, seg, c, n1g, n1s, wd, db, n2g, n2s, wc, cb, n3g, n3s, wu, ub):
    micro, length, width, inner, taps = z.micro, z.length, z.width, z.inner, z.taps
    rows = lambda last, kind: pltpu.VMEM((micro, length, last), kind)
    job_scratch = []
    n = {"c": 2, "x": z.seq // 2, "y": 2, "z": z.rows // 2}
    for name in JOBS:
        block = z.blocks()[name]
        lead = tuple(n[d] for d in ("c",) + ORDERS[name])
        most = max(max(lead) - 1, 1)
        job_scratch.append(pltpu.VMEM(lead + block, bf16))
        for stage in range(4):
            job_scratch.append(pltpu.VMEM((lead[stage] - 1,) + lead[stage + 1 :] + block, bf16))
        job_scratch += [pltpu.SemaphoreType.DMA((4, most))] * 2
    wide = max(z.seq, z.rows)
    scratch = [
        rows(width, bf16),
        rows(width, bf16),
        pltpu.VMEM((width, inner), bf16),
        pltpu.VMEM((taps, inner, inner), bf16),
        pltpu.VMEM((inner, width), bf16),
        rows(width, bf16),
        rows(width, bf16),
        pltpu.VMEM((2, micro, length, 128), f32),
        rows(inner, bf16),
        rows(128, f32),
        rows(inner, bf16),
        pltpu.VMEM((micro, 3 * length, inner), bf16),
        pltpu.VMEM((micro, 3 * length, inner), bf16),
        pltpu.VMEM((taps, micro, length, 128), bf16),
        rows(inner, bf16),
        rows(inner, bf16),
        rows(width, bf16),
        pltpu.VMEM((inner, width), f32),
        pltpu.VMEM((8, length), jnp.int32),
        pltpu.VMEM((2, 8, length), jnp.int32),
        pltpu.VMEM((3, 8, width), f32),
        pltpu.VMEM((6, 8, inner), f32),
        pltpu.VMEM((2, 8, inner), f32),
        pltpu.VMEM((2, 8, inner), f32),
        pltpu.VMEM((2, z.seq, 8, inner), f32),
        pltpu.VMEM((2, z.rows, 8, inner), f32),
        pltpu.SemaphoreType.DMA((2 * micro + 3,)),
        pltpu.SemaphoreType.DMA((2 * micro,)),
        pltpu.SemaphoreType.DMA((2, 2, micro)),
        pltpu.SemaphoreType.DMA((2, 2, micro)),
        pltpu.SemaphoreType.DMA((2,)),
        pltpu.SemaphoreType.DMA((2,)),
        pltpu.SemaphoreType.DMA((2, 2, wide)),
        pltpu.SemaphoreType.DMA((2, 2, wide)),
    ] + job_scratch
    flat = lambda v: v.reshape(1, -1)
    out, ig, vectors, down, conv, up = pl.pallas_call(
        functools.partial(kernel, z),
        out_shape=(
            jax.ShapeDtypeStruct(x.shape, bf16),
            jax.ShapeDtypeStruct(x.shape, bf16),
            jax.ShapeDtypeStruct((16, inner), f32),
            jax.ShapeDtypeStruct(z.down, f32),
            jax.ShapeDtypeStruct((taps,) + z.conv, f32),
            jax.ShapeDtypeStruct(z.up, f32),
        ),
        in_specs=[ANY, VMEM, ANY, VMEM, VMEM, ANY, VMEM, VMEM, VMEM, ANY, VMEM, VMEM, VMEM, ANY, VMEM],
        out_specs=(ANY, ANY, VMEM, VMEM, VMEM, VMEM),
        scratch_shapes=scratch,
        compiler_params=pltpu.CompilerParams(
            collective_id=0, has_side_effects=True, vmem_limit_bytes=62 << 20
        ),
    )(
        x, seg, c, flat(n1g), flat(n1s), wd, flat(db), flat(n2g), flat(n2s), wc, flat(cb),
        flat(n3g), flat(n3s), wu, flat(ub),
    )
    whole = lambda k: vectors[k : k + 2].reshape(-1)
    return (
        out, ig, whole(8), whole(10), down, vectors[7], vectors[5], vectors[6], conv, vectors[4],
        vectors[2], vectors[3], up, whole(0),
    )


def solution(mesh):
    def step(*args):
        micro, length, width = args[0].shape
        taps, inner, _ = args[9].shape
        z = Sizes(mesh.shape["rows"], mesh.shape["seq"], micro, length, width, inner, taps)
        return per_device(z, *args)

    rows = P("rows", "seq", None)
    matrix = P("rows", "seq")
    return jax.shard_map(
        step,
        mesh=mesh,
        in_specs=(rows, matrix, rows) + (P(),) * 12,
        out_specs=(rows, rows, P(), P(), matrix, P(), P(), P(), P(None, "rows", "seq"))
        + (P(),) * 3
        + (matrix, P()),
        check_vma=False,
    )
```

```python
import functools
import math

import jax
import jax.numpy as jnp
from jax import lax
from jax.experimental import pallas as pl
from jax.experimental.pallas import tpu as pltpu
from jax.sharding import PartitionSpec as P

DILATION = 128
EPSILON = 1e-05
MESH = pl.DeviceIdType.MESH
SLICES = 4
bf16 = jnp.bfloat16
f32 = jnp.float32
ANY = pl.BlockSpec(memory_space=pl.ANY)
VMEM = pl.BlockSpec(memory_space=pltpu.VMEM)


def up_to(value, step):
    return -(-value // step) * step


def normalise(values):
    mean = jnp.mean(values, axis=-1, keepdims=True)
    centred = values - mean
    scale = lax.rsqrt(jnp.mean(centred * centred, axis=-1, keepdims=True) + EPSILON)
    return mean, scale, centred * scale


def gelu_and_slope(values):
    phi = 0.5 + 0.5 * lax.erf(values * math.sqrt(0.5))
    density = jnp.exp(-0.5 * values * values) * (1.0 / math.sqrt(2.0 * math.pi))
    return values * phi, phi + values * density


def norm_back(grad, normal, scale):
    mean = jnp.mean(grad, axis=-1, keepdims=True)
    along = jnp.mean(grad * normal, axis=-1, keepdims=True)
    return scale * (grad - mean - normal * along)


def fold(values):
    rows, width = values.shape
    return jnp.sum(values.reshape(rows // 8, 8, width), axis=0)


def dot(left, right):
    return jnp.dot(left, right, preferred_element_type=f32)


def dot_rows(left, right):
    return lax.dot_general(left, right, (((0,), (0,)), ((), ())), preferred_element_type=f32)


def dot_cols(left, right):
    return lax.dot_general(left, right, (((1,), (1,)), ((), ())), preferred_element_type=f32)


class Row:
    def __init__(self, ref):
        self.ref = ref

    def __getitem__(self, _):
        return self.ref[...].reshape(1, -1)


class Place:
    def __init__(self, rows, seq):
        self.rows, self.seq = rows, seq
        self.r, self.s = lax.axis_index("rows"), lax.axis_index("seq")
        self.size = sizes_of(rows, seq)
        z = lax.div(self.r, 2)
        self.at = {
            "c": lax.rem(self.s, 2),
            "x": lax.div(self.s, 2),
            "y": lax.rem(self.r, 2),
            "z": z,
            "p": lax.rem(z, 2),
            "q": lax.div(z, 2),
        }

    def peer(self, dim, index):
        at = dict(self.at)
        at[dim] = index
        z = at["q"] * 2 + at["p"] if dim in "pq" else at["z"]
        return (z * 2 + at["y"], at["x"] * 2 + at["c"])


def sizes_of(rows, seq):
    return {"c": 2, "x": seq // 2, "y": 2, "z": rows // 2, "p": 2, "q": rows // 4}


def split(index):
    if isinstance(index, int):
        return index // 2, index % 2
    return lax.div(index, 2), lax.rem(index, 2)


class Reduction:
    def __init__(self, place, order, send, got, send_sem, recv_sem):
        self.place, self.order = place, "c" + order
        self.send, self.got, self.send_sem, self.recv_sem = send, got, send_sem, recv_sem
        self.at = [place.at[d] for d in self.order]
        self.size = [place.size[d] for d in self.order]

    def index(self, r, s):
        z, y = split(r)
        q, p = split(z)
        where = {"c": s % 2, "x": s // 2, "y": y, "z": z, "p": p, "q": q}
        return tuple(where[d] for d in self.order)

    def copies(self, stage):
        n, at = self.size[stage], self.at[stage]
        base = sum(self.size[:stage]) - stage
        found = []
        for off in range(1, n):
            other = lax.rem(at + off, n)
            slot = n - 1 - off
            found.append(
                (
                    other,
                    functools.partial(
                        pltpu.make_async_remote_copy,
                        src_ref=self.send.at[tuple(self.at[:stage]) + (other,)],
                        dst_ref=self.got[stage].at[slot],
                        send_sem=self.send_sem.at[base + slot],
                        recv_sem=self.recv_sem.at[base + slot],
                        device_id=self.place.peer(self.order[stage], other),
                        device_id_type=MESH,
                    ),
                )
            )
        return found

    def total(self, stage, prefix, rest):
        value = self.send[tuple(prefix) + rest].astype(f32)
        for s in range(stage):
            for slot in range(self.size[s] - 1):
                value = value + self.got[s][(slot,) + tuple(prefix[s + 1 :]) + rest].astype(f32)
        return value

    def start(self):
        for _, copy in self.copies(0):
            copy().start()

    def step(self, stage):
        for _, copy in self.copies(stage - 1):
            copy().wait_recv()
        for other, copy in self.copies(stage):
            prefix = self.at[:stage] + [other]
            lead = self.size[stage + 1 :]
            if not lead:
                self.send[tuple(prefix)] = self.total(stage, prefix, ()).astype(bf16)
            else:
                count = math.prod(lead)

                def add(i, carry, prefix=prefix, lead=lead):
                    rest = []
                    for n in reversed(lead):
                        rest.insert(0, lax.rem(i, n))
                        i = lax.div(i, n)
                    rest = tuple(rest)
                    self.send[tuple(prefix) + rest] = self.total(stage, prefix, rest).astype(bf16)
                    return carry

                lax.fori_loop(0, count, add, 0)
            copy().start()

    def finish(self):
        last = len(self.order) - 1
        for _, copy in self.copies(last):
            copy().wait_recv()
        return self.total(last + 1, self.at, ())

    def drain(self):
        for stage in range(len(self.order)):
            for _, copy in self.copies(stage):
                copy().wait_send()


JOBS = {
    "up": ("yxz", (("up", 0, 0, 10),)),
    "conv0": ("pyxq", (("conv", 0, 0, 8),)),
    "conv1": ("xyz", (("conv", 0, 8, 10), ("conv", 1, 0, 6))),
    "conv2": ("pxyq", (("conv", 1, 6, 10), ("conv", 2, 0, 4))),
    "conv3": ("ypxq", (("conv", 2, 4, 10),)),
    "conv4": ("xypq", (("conv", 3, 0, 8),)),
    "conv5": ("pyxq", (("conv", 3, 8, 10), ("conv", 4, 0, 10))),
    "down0": ("xyz", (("down", 0, 0, 4),)),
    "down1": ("yxz", (("down", 0, 4, 7),)),
    "down2": ("yxz", (("down", 0, 7, 10),)),
}


class Sizes:
    def __init__(self, rows, seq, micro, length, width, inner, taps):
        self.rows, self.seq = rows, seq
        self.micro, self.length, self.width, self.inner, self.taps = micro, length, width, inner, taps
        self.positions = micro * length
        self.margin = taps // 2 * DILATION
        assert self.margin <= length
        self.share = {
            "up": (inner // rows, width // seq),
            "conv": (inner // rows, inner // seq),
            "down": (inner // seq, width // rows),
        }
        self.unroll = rows * seq <= 32
        assert width == 2 * inner and micro % 2 == 0 and micro // 2 * length <= inner and taps == 5

    def groups(self, matrix, begin, end):
        count = up_to(self.share[matrix][0], 16) // 16
        return range(count * begin // 10, count * end // 10)

    def lanes(self, name):
        found, lane = [], 0
        for matrix, tap, begin, end in JOBS[name][1]:
            for group in self.groups(matrix, begin, end):
                found.append((matrix, tap, group, lane))
                lane += self.share[matrix][1]
        return found, lane

    def block(self, name):
        return (16, up_to(self.lanes(name)[1], 128))


def kernel(sizes, *refs):
    (
        x_hbm, seg, c_hbm, n1g, n1s, wd_hbm, db, n2g, n2s, wc_hbm, cb, n3g, n3s, wu_hbm, ub,
        x, c, vec_out, down_out, conv_out, up_out,
        wd, wc, wu, first, slope1, stat1, normal2, scale2, slope2, sext, gext, masks,
        third, masked, held, product, own_labels, labels,
        down_turned, sum1, sum2,
        own_early, got_early, part_early, far_early, total_early, own_late, got_late, part_late, far_late, total_late,
        load_sem, halo_send, halo_recv, label_send, label_recv, *rest,
    ) = refs
    z = sizes
    vec_sems, job_refs = rest[:8], rest[8:]
    vector_refs = (
        own_early, got_early, part_early, far_early, total_early, own_late, got_late, part_late, far_late, total_late,
    )
    n1g, n1s, db, n2g, n2s, cb, n3g, n3s, ub = (
        Row(ref) for ref in (n1g, n1s, db, n2g, n2s, cb, n3g, n3s, ub)
    )
    micro, length, width, inner, taps = z.micro, z.length, z.width, z.inner, z.taps
    place = Place(z.rows, z.seq)
    me_r, me_s = place.r, place.s
    has_left, has_right = me_s > 0, me_s < z.seq - 1
    left = (me_r, jnp.maximum(me_s - 1, 0))
    right = (me_r, jnp.minimum(me_s + 1, z.seq - 1))
    jobs = {}
    for name, (order, _) in JOBS.items():
        send, *got, send_sem, recv_sem = job_refs[: len(order) + 4]
        job_refs = job_refs[len(order) + 4 :]
        jobs[name] = Reduction(place, order, send, got, send_sem, recv_sem)

    def steps(*wanted):
        for name, stage in wanted:
            jobs[name].step(stage)

    def load_rows(source, target, base, i):
        return pltpu.make_async_copy(source.at[i], target.at[i], load_sem.at[base + i])

    weight_loads = [
        pltpu.make_async_copy(source, target, load_sem.at[2 * micro + k])
        for k, (source, target) in enumerate(((wd_hbm, wd), (wu_hbm, wu), (wc_hbm, wc)))
    ]
    load_rows(x_hbm, x, 0, 0).start()
    weight_loads[0].start()
    for i in range(1, micro):
        load_rows(x_hbm, x, 0, i).start()
    for i in range(micro):
        load_rows(c_hbm, c, micro, i).start()
    weight_loads[1].start()
    weight_loads[2].start()

    barrier = pltpu.get_barrier_semaphore()
    for off in range(1, z.seq):
        pl.semaphore_signal(
            barrier, inc=1, device_id=(me_r, lax.rem(me_s + off, z.seq)), device_id_type=MESH
        )
    for off in range(1, z.rows):
        pl.semaphore_signal(
            barrier, inc=1, device_id=(lax.rem(me_r + off, z.rows), me_s), device_id_type=MESH
        )

    own_labels[...] = jnp.zeros(own_labels.shape, jnp.int32)
    own_labels[0:micro, :] = seg[...]
    sum1[...] = jnp.zeros(sum1.shape, f32)
    sum2[...] = jnp.zeros(sum2.shape, f32)

    @pl.when(jnp.logical_not(has_left))
    def _():
        labels[0] = jnp.full(labels.shape[1:], -1, jnp.int32)
        sext[:, 0:length, :] = jnp.zeros((micro, length, inner), bf16)
        gext[:, 0:length, :] = jnp.zeros((micro, length, inner), bf16)

    @pl.when(jnp.logical_not(has_right))
    def _():
        labels[1] = jnp.full(labels.shape[1:], -1, jnp.int32)
        sext[:, 2 * length :, :] = jnp.zeros((micro, length, inner), bf16)
        gext[:, 2 * length :, :] = jnp.zeros((micro, length, inner), bf16)

    def halo(ext, turn, i):
        return (
            (
                has_right,
                pltpu.make_async_remote_copy(
                    src_ref=ext.at[i, pl.ds(length, length)],
                    dst_ref=ext.at[i, pl.ds(0, length)],
                    send_sem=halo_send.at[turn, 0, i],
                    recv_sem=halo_recv.at[turn, 0, i],
                    device_id=right,
                    device_id_type=MESH,
                ),
            ),
            (
                has_left,
                pltpu.make_async_remote_copy(
                    src_ref=ext.at[i, pl.ds(length, length)],
                    dst_ref=ext.at[i, pl.ds(2 * length, length)],
                    send_sem=halo_send.at[turn, 1, i],
                    recv_sem=halo_recv.at[turn, 1, i],
                    device_id=left,
                    device_id_type=MESH,
                ),
            ),
        )

    def label_copies():
        return [
            (
                ok,
                pltpu.make_async_remote_copy(
                    src_ref=own_labels,
                    dst_ref=labels.at[way],
                    send_sem=label_send.at[way],
                    recv_sem=label_recv.at[way],
                    device_id=target,
                    device_id_type=MESH,
                ),
            )
            for way, (ok, target) in enumerate(((has_right, right), (has_left, left)))
        ]

    def start_all(copies):
        for ok, copy in copies:
            pl.when(ok)(copy.start)

    def wait_sent(copies):
        for ok, copy in copies:
            pl.when(ok)(copy.wait_send)

    def wait_got(copies):
        pl.when(has_left)(copies[0][1].wait_recv)
        pl.when(has_right)(copies[1][1].wait_recv)

    def first_half(i):
        chunk = min(128, length)
        for begin in range(0, length, chunk):
            some = pl.ds(begin, chunk)
            mean, scale, normal = normalise(x[i, some, :].astype(f32))
            act, slope = gelu_and_slope(normal * n1g[...] + n1s[...])
            first[i, some, :] = act.astype(bf16)
            slope1[i, some, :] = slope.astype(bf16)
            stat1[0, i, some, :] = jnp.broadcast_to(mean, (chunk, 128))
            stat1[1, i, some, :] = jnp.broadcast_to(scale, (chunk, 128))

    def second_half(i, reduced):
        _, scale, normal = normalise(reduced)
        act, slope = gelu_and_slope(normal * n2g[...] + n2s[...])
        sext[i, pl.ds(length, length), :] = act.astype(bf16)
        slope2[i] = slope.astype(bf16)
        normal2[i] = normal.astype(bf16)
        scale2[i] = jnp.broadcast_to(scale, (length, 128))

    def repeat(count, body):
        if z.unroll:
            for i in range(count):
                body(i)
        else:
            lax.fori_loop(0, count, lambda i, carry: (body(i), carry)[1], 0)

    for name, job in jobs.items():
        used, lanes = z.lanes(name)[1], job.send.shape[-1]
        if used < lanes:
            job.send[..., used:] = jnp.zeros(job.send.shape[:-1] + (lanes - used,), bf16)
    load_rows(x_hbm, x, 0, 0).wait()
    first_half(0)
    weight_loads[0].wait()

    def head(i, carry):
        load_rows(x_hbm, x, 0, i + 1).wait()
        reduced = dot(first[i], wd[...]) + db[...]
        first_half(i + 1)
        second_half(i, reduced)

        @pl.when(i == 0)
        def _():
            pl.semaphore_wait(barrier, z.seq + z.rows - 2)
            start_all(label_copies())

        start_all(halo(sext, 0, i))
        return carry

    lax.fori_loop(0, micro - 1, head, 0)
    second_half(micro - 1, dot(first[micro - 1], wd[...]) + db[...])
    start_all(halo(sext, 0, micro - 1))

    def third_grad_at(i):
        row, column = split(i)
        return (
            pl.ds(pl.multiple_of(row * length, 128), length),
            pl.ds(pl.multiple_of(column * inner, 128), inner),
        )

    weight_loads[1].wait()

    def third_back(i, carry):
        load_rows(c_hbm, c, micro, i).wait()
        product[third_grad_at(i)] = dot_cols(c[i], wu[...])
        sum1[0] += fold(c[i].astype(f32))
        return carry

    lax.fori_loop(0, micro, third_back, 0)

    wait_got(label_copies())
    spread = jnp.concatenate([labels[0], own_labels[...], labels[1]], axis=1).astype(f32).T
    for i in range(micro):
        column = spread[:, i : i + 1]
        centre = column[length : 2 * length]
        for n, k in enumerate(k for k in range(taps) if k != taps // 2):
            begin = length - z.margin + k * DILATION
            same = (column[begin : begin + length] == centre).astype(f32)
            masks[n, i] = jnp.broadcast_to(same, (length, 128)).astype(bf16)

    def tap_of(ext, i, k):
        begin = length - z.margin + k * DILATION
        block = ext[i, pl.ds(begin, length), :]
        if k == taps // 2:
            return block
        keep = masks[k if k < taps // 2 else k - 1, i]
        return block * jnp.concatenate([keep] * (inner // 128), axis=1)

    weight_loads[2].wait()

    def convolve(i, beside=lambda part: None):
        conv = cb[...]
        for k in range(taps):
            conv = conv + dot(tap_of(sext, i, k), wc[k])
            beside(k)
        return conv.astype(bf16)

    parts = [pl.ds(begin, length // 4) for begin in range(0, length, length // 4)]

    def middle(i, part):
        if part >= len(parts):
            return
        some = parts[part]
        mixed = held[some, :].astype(f32)
        _, scale, normal = normalise(mixed)
        act, slope = gelu_and_slope(normal * n3g[...] + n3s[...])
        third[i, some, :] = act.astype(bf16)
        row, column = third_grad_at(i)
        grad = product[pl.ds(row.start + some.start, some.size), column] * slope
        sum2[0] += fold(grad * normal)
        sum2[1] += fold(grad)
        mixed_grad = norm_back(grad * n3g[...], normal, scale).astype(bf16)
        gext[i, pl.ds(length + some.start, some.size), :] = mixed_grad
        sum2[2] += fold(mixed_grad.astype(f32))

    wait_got(halo(sext, 0, 0))
    held[...] = convolve(0)

    def middle_step(i, carry):
        wait_got(halo(sext, 0, i + 1))
        held[...] = convolve(i + 1, lambda part: middle(i, part))
        start_all(halo(gext, 1, i))
        return carry

    lax.fori_loop(0, micro - 1, middle_step, 0)
    for part in range(len(parts)):
        middle(micro - 1, part)
    start_all(halo(gext, 1, micro - 1))

    whole = lambda ref: ref[...].reshape(z.positions, ref.shape[-1])
    own = lambda ext: ext[:, length : 2 * length, :].reshape(z.positions, inner)

    def pack(matrix, tap, base, rows_over):
        share = z.share[matrix]
        over_rows, over_columns = (z.rows, z.seq) if rows_over == "rows" else (z.seq, z.rows)
        targets = [
            (job, group, lane)
            for name, job in jobs.items()
            for m, t, group, lane in z.lanes(name)[0]
            if (m, t) == (matrix, tap)
        ]

        def pack_rows(k):
            begin = k * share[0]
            if not isinstance(k, int):
                begin = pl.multiple_of(begin, 8)
            rows = product[pl.ds(begin, share[0]), base : base + over_columns * share[1]]
            for j in range(over_columns):
                piece = rows[:, j * share[1] : (j + 1) * share[1]]
                for job, group, lane in targets:
                    at = job.index(k, j) if rows_over == "rows" else job.index(j, k)
                    some = piece[16 * group : min(16 * group + 16, share[0])]
                    short = 16 - some.shape[0]
                    if short:
                        some = jnp.concatenate([some, jnp.zeros((short, share[1]), f32)], axis=0)
                    job.send[at + (slice(None), pl.ds(lane, share[1]))] = some.astype(bf16)

        repeat(over_rows, pack_rows)

    def conv_weight_grad(k):
        if k == taps // 2:
            source = own(sext)
        else:
            for i in range(micro):
                masked[i] = tap_of(sext, i, k)
            source = whole(masked)
        base = k % 2 * inner
        product[:, base : base + inner] = dot_rows(source, own(gext))
        pack("conv", k, base, "rows")

    product[...] = dot_rows(whole(third), whole(c))
    pack("up", 0, 0, "rows")
    jobs["up"].start()
    conv_weight_grad(0)
    jobs["conv0"].start()
    conv_weight_grad(1)
    jobs["conv1"].start()
    steps(("up", 1), ("conv0", 1))
    conv_weight_grad(2)
    jobs["conv2"].start()
    jobs["conv3"].start()
    steps(("conv1", 1))
    conv_weight_grad(3)
    jobs["conv4"].start()
    steps(("conv2", 1))
    conv_weight_grad(4)
    jobs["conv5"].start()
    steps(("conv3", 1), ("conv4", 1), ("conv0", 2))

    def convolve_back(i, beside=lambda part: None):
        grad = dot_cols(tap_of(gext, i, 0), wc[taps - 1])
        beside(0)
        for k in range(1, taps):
            grad = grad + dot_cols(tap_of(gext, i, k), wc[taps - 1 - k])
            beside(k)
        return grad.astype(bf16)

    def second_back(i, part):
        if part >= len(parts):
            return
        some = parts[part]
        grad = held[some, :].astype(f32) * slope2[i, some, :].astype(f32)
        normal = normal2[i, some, :].astype(f32)
        sum2[3] += fold(grad * normal)
        sum2[4] += fold(grad)
        scale = jnp.concatenate([scale2[i, some, :]] * (inner // 128), axis=1)
        reduced_grad = norm_back(grad * n2g[...], normal, scale).astype(bf16)
        sext[i, some, :] = reduced_grad
        sum2[5] += fold(reduced_grad.astype(f32))

    wait_got(halo(gext, 1, 0))
    held[...] = convolve_back(0)
    steps(("conv1", 2), ("conv5", 1))

    def conv_back_step(i, carry):
        wait_got(halo(gext, 1, i + 1))
        held[...] = convolve_back(i + 1, lambda part: second_back(i, part))

        @pl.when(i == 0)
        def _():
            steps(("conv2", 2))

        @pl.when(i == 1)
        def _():
            steps(("up", 2), ("conv4", 2))

        return carry

    lax.fori_loop(0, micro - 1, conv_back_step, 0)
    for part in range(len(parts)):
        second_back(micro - 1, part)
    steps(("conv3", 2))

    reduced_grads = sext[:, 0:length, :].reshape(z.positions, inner)
    product[...] = dot_rows(reduced_grads, whole(first))
    pack("down", 0, 0, "seq")
    for name in ("down0", "down1", "down2"):
        jobs[name].start()
    half = width // 2

    group, mine = lax.div(me_s, SLICES) * SLICES, lax.rem(me_s, SLICES)

    def vector_copies(turn, stage):
        own, got, part, far, total = vector_refs[5 * turn : 5 * turn + 5]
        me, count = ((me_s, z.seq), (me_r, z.rows), (mine, SLICES))[stage]
        base = (0, z.seq, z.seq + z.rows)[stage]
        sends, gets = [], []
        for off in range(1, count):
            other = lax.rem(me + off, count)
            target = ((me_r, other), (other, me_s), (me_r, group + other))[stage]
            source = (own.at[lax.rem(other, SLICES)], part, total.at[mine])[stage]
            for found, slot in ((sends, me), (gets, other)):
                found.append(
                    functools.partial(
                        pltpu.make_async_remote_copy,
                        src_ref=source,
                        dst_ref=(got, far, total)[stage].at[slot],
                        send_sem=vec_sems[4 * turn].at[base + off],
                        recv_sem=vec_sems[4 * turn + 1 + stage].at[slot],
                        device_id=target,
                        device_id_type=MESH,
                    )
                )
        return sends, gets

    def vector_start(turn, stage):
        for copy in vector_copies(turn, stage)[0]:
            copy().start()

    def vector_sent(turn):
        for stage in range(3):
            for copy in vector_copies(turn, stage)[0]:
                copy().wait_send()

    def vector_step(turn, stage):
        own, got, part, far, total = vector_refs[5 * turn : 5 * turn + 5]
        for copy in vector_copies(turn, stage - 1)[1]:
            copy().wait_recv()
        if stage == 3:
            rows = own.shape[1]
            for k in range(SLICES):
                begin = (0, 8)[turn] + k * rows
                vec_out[begin : begin + rows, :] = total[k]
            return
        me, count = ((me_s, z.seq), (me_r, z.rows))[stage - 1]
        inbox = (got, far)[stage - 1]
        inbox[me] = (own[mine], part[...])[stage - 1]
        value = inbox[0]
        for k in range(1, count):
            value = value + inbox[k]
        if stage == 1:
            part[...] = value
        else:
            total[mine] = value
        vector_start(turn, stage)

    def squeeze(value):
        return jnp.sum(value, axis=0, keepdims=True)

    early = [squeeze(sum1[0, :, h * half : (h + 1) * half]) for h in range(2)]
    early += [squeeze(sum2[k]) for k in range(6)]
    for k, row in enumerate(early):
        vector_refs[0][k // 2, k % 2 : k % 2 + 1, :] = row
    vector_start(0, 0)

    steps(("conv2", 3), ("conv0", 3), ("conv5", 2), ("conv1", 3))

    def first_back(i, carry):
        grads = dot_cols(sext[i, pl.ds(0, length), :], wd[...])
        chunk = min(128, length)
        for begin in range(0, length, chunk):
            some = pl.ds(begin, chunk)
            grad = grads[begin : begin + chunk] * slope1[i, some, :].astype(f32)
            mean = jnp.concatenate([stat1[0, i, some, :]] * (width // 128), axis=1)
            scale = jnp.concatenate([stat1[1, i, some, :]] * (width // 128), axis=1)
            normal = (x[i, some, :].astype(f32) - mean) * scale
            sum1[1] += fold(grad * normal)
            sum1[2] += fold(grad)
            part = norm_back(grad * n1g[...], normal, scale)
            c[i, some, :] = (c[i, some, :].astype(f32) + part).astype(bf16)

        @pl.when(i == 0)
        def _():
            steps(("conv3", 3), ("up", 3), ("conv4", 3), ("down0", 1), ("down1", 1), ("conv2", 4), ("down2", 1))

        @pl.when(i == 1)
        def _():
            steps(("conv0", 4))
            vector_step(0, 1)

        @pl.when(i == 2)
        def _():
            steps(("conv3", 4), ("conv5", 3))

        return carry

    lax.fori_loop(0, micro, first_back, 0)
    late = [squeeze(sum1[k, :, h * half : (h + 1) * half]) for k in (1, 2) for h in range(2)]
    for k, row in enumerate(late):
        vector_refs[5][k] = row
    vector_start(1, 0)

    def finish_output(i, carry):
        x[i] = (x[i].astype(f32) + dot(third[i], wu[...]) + ub[...]).astype(bf16)

        @pl.when(i == 1)
        def _():
            steps(("down1", 2), ("down0", 2))

        @pl.when(i == 2)
        def _():
            steps(("conv4", 4))

        return carry

    lax.fori_loop(0, micro, finish_output, 0)
    steps(("conv5", 4))
    vector_step(0, 2)
    vector_step(1, 1)

    def finish(name):
        value = jobs[name].finish()
        for matrix, tap, group, lane in z.lanes(name)[0]:
            rows, columns = z.share[matrix]
            target = {"up": up_out, "conv": conv_out.at[tap], "down": down_turned}[matrix]
            count = min(16, rows - 16 * group)
            target[pl.ds(16 * group, count), :] = value[:count, lane : lane + columns]

    for name in ("conv1", "up", "conv2", "conv0"):
        finish(name)
    steps(("down2", 2))
    for i in range(micro):
        wait_sent(halo(sext, 0, i))
        wait_sent(halo(gext, 1, i))
    wait_sent(label_copies())
    finish("conv3")
    steps(("down1", 3))
    finish("conv4")
    steps(("down0", 3))
    for name in ("up", "conv0", "conv1", "conv2", "conv3", "conv4"):
        jobs[name].drain()
    vector_step(1, 2)
    finish("conv5")
    steps(("down2", 3))
    vector_step(0, 3)
    vector_sent(0)
    vector_step(1, 3)
    for name in ("down1", "down0", "down2"):
        finish(name)
    down_out[...] = down_turned[...].T

    vector_sent(1)
    for name in ("conv5", "down0", "down1", "down2"):
        jobs[name].drain()


def per_device(z, x, seg, c, n1g, n1s, wd, db, n2g, n2s, wc, cb, n3g, n3s, wu, ub):
    micro, length, width, inner, taps = z.micro, z.length, z.width, z.inner, z.taps
    rows = lambda last, kind: pltpu.VMEM((micro, length, last), kind)
    job_scratch = []
    n = sizes_of(z.rows, z.seq)
    for name, (order, _) in JOBS.items():
        block = z.block(name)
        lead = tuple(n[d] for d in "c" + order)
        job_scratch.append(pltpu.VMEM(lead + block, bf16))
        for stage in range(len(lead)):
            job_scratch.append(pltpu.VMEM((lead[stage] - 1,) + lead[stage + 1 :] + block, bf16))
        job_scratch += [pltpu.SemaphoreType.DMA((sum(lead) - len(lead),))] * 2
    scratch = [
        pltpu.VMEM((width, inner), bf16),
        pltpu.VMEM((taps, inner, inner), bf16),
        pltpu.VMEM((inner, width), bf16),
        rows(width, bf16),
        rows(width, bf16),
        pltpu.VMEM((2, micro, length, 128), f32),
        rows(inner, bf16),
        rows(128, f32),
        rows(inner, bf16),
        pltpu.VMEM((micro, 3 * length, inner), bf16),
        pltpu.VMEM((micro, 3 * length, inner), bf16),
        pltpu.VMEM((taps - 1, micro, length, 128), bf16),
        rows(inner, bf16),
        rows(inner, bf16),
        pltpu.VMEM((length, inner), bf16),
        pltpu.VMEM((inner, width), f32),
        pltpu.VMEM((8, length), jnp.int32),
        pltpu.VMEM((2, 8, length), jnp.int32),
        pltpu.VMEM(z.share["down"], f32),
        pltpu.VMEM((3, 8, width), f32),
        pltpu.VMEM((6, 8, inner), f32),
    ] + [
        pltpu.VMEM(lead + (rows_of, inner), f32)
        for rows_of in (2, 1)
        for lead in ((SLICES,), (z.seq,), (), (z.rows,), (SLICES,))
    ] + [
        pltpu.SemaphoreType.DMA((2 * micro + 3,)),
        pltpu.SemaphoreType.DMA((2, 2, micro)),
        pltpu.SemaphoreType.DMA((2, 2, micro)),
        pltpu.SemaphoreType.DMA((2,)),
        pltpu.SemaphoreType.DMA((2,)),
    ] + [
        pltpu.SemaphoreType.DMA((count,))
        for _ in range(2)
        for count in (z.seq + z.rows + SLICES, z.seq, z.rows, SLICES)
    ] + job_scratch
    out, ig, vectors, down, conv, up = pl.pallas_call(
        functools.partial(kernel, z),
        out_shape=(
            pltpu.VMEM(x.shape, bf16),
            pltpu.VMEM(x.shape, bf16),
            pltpu.VMEM((16, inner), f32),
            pltpu.VMEM(z.share["down"][::-1], f32),
            pltpu.VMEM((taps,) + z.share["conv"], f32),
            pltpu.VMEM(z.share["up"], f32),
        ),
        in_specs=[ANY, VMEM, ANY, VMEM, VMEM, ANY, VMEM, VMEM, VMEM, ANY, VMEM, VMEM, VMEM, ANY, VMEM],
        out_specs=(VMEM,) * 6,
        scratch_shapes=scratch,
        compiler_params=pltpu.CompilerParams(
            collective_id=0, has_side_effects=True, vmem_limit_bytes=58 << 20
        ),
    )(
        x, seg, c, n1g, n1s, wd, db, n2g, n2s, wc, cb, n3g, n3s, wu, ub,
    )
    vector = lambda n: jax.ShapeDtypeStruct((n,), f32)
    out, ig, down, conv, up, *vectors = pl.pallas_call(
        write_out,
        out_shape=(
            jax.ShapeDtypeStruct(x.shape, bf16),
            jax.ShapeDtypeStruct(x.shape, bf16),
            jax.ShapeDtypeStruct(z.share["down"][::-1], f32),
            jax.ShapeDtypeStruct((taps,) + z.share["conv"], f32),
            jax.ShapeDtypeStruct(z.share["up"], f32),
        )
        + tuple(vector(width if first + 1 < last else inner) for first, last in VECTORS),
        in_specs=[VMEM] * 6,
        out_specs=(ANY,) * (5 + len(VECTORS)),
        scratch_shapes=[pltpu.VMEM((width if first + 1 < last else inner,), f32) for first, last in VECTORS]
        + [pltpu.SemaphoreType.DMA((5 + len(VECTORS),))],
        compiler_params=pltpu.CompilerParams(vmem_limit_bytes=2 << 20),
    )(*(pltpu.with_memory_space_constraint(v, pltpu.VMEM) for v in (out, ig, vectors, down, conv, up)))
    ub, n3g, n3s, cb, n2g, n2s, db, n1g, n1s = vectors
    return out, ig, n1g, n1s, down, db, n2g, n2s, conv, cb, n3g, n3s, up, ub


VECTORS = ((0, 2), (2, 3), (3, 4), (4, 5), (5, 6), (6, 7), (7, 8), (8, 10), (10, 12))


def write_out(out, ig, vectors, down, conv, up, *rest):
    count = len(VECTORS)
    targets, rows, sem = rest[: 5 + count], rest[5 + count : -1], rest[-1]
    width = vectors.shape[1]
    sources = (out, ig, down, conv, up) + rows
    copies = [
        pltpu.make_async_copy(source, target, sem.at[k])
        for k, (source, target) in enumerate(zip(sources, targets))
    ]
    for copy in copies[:5]:
        copy.start()
    for row, (begin, end) in zip(rows, VECTORS):
        for k in range(begin, end):
            row[pl.ds((k - begin) * width, width)] = vectors[k, :]
    for copy in copies[5:]:
        copy.start()
    for copy in copies:
        copy.wait()


def solution(mesh):
    def step(*args):
        micro, length, width = args[0].shape
        taps, inner, _ = args[9].shape
        z = Sizes(mesh.shape["rows"], mesh.shape["seq"], micro, length, width, inner, taps)
        return per_device(z, *args)

    rows = P("rows", "seq", None)
    matrix = P("rows", "seq")
    return jax.shard_map(
        step,
        mesh=mesh,
        in_specs=(rows, matrix, rows) + (P(),) * 12,
        out_specs=(rows, rows, P(), P(), matrix, P(), P(), P(), P(None, "rows", "seq"))
        + (P(),) * 3
        + (matrix, P()),
        check_vma=False,
    )
```

```python
import functools
import math

import jax
import jax.numpy as jnp
from jax import lax
from jax.experimental import pallas as pl
from jax.experimental.pallas import tpu as pltpu
from jax.sharding import PartitionSpec as P

DILATION = 128
EPSILON = 1e-05
MESH = pl.DeviceIdType.MESH
SLICES = 4
bf16 = jnp.bfloat16
f32 = jnp.float32
ANY = pl.BlockSpec(memory_space=pl.ANY)
VMEM = pl.BlockSpec(memory_space=pltpu.VMEM)


def up_to(value, step):
    return -(-value // step) * step


def normalise(values):
    mean = jnp.mean(values, axis=-1, keepdims=True)
    centred = values - mean
    scale = lax.rsqrt(jnp.mean(centred * centred, axis=-1, keepdims=True) + EPSILON)
    return mean, scale, centred * scale


def gelu_and_slope(values):
    phi = 0.5 + 0.5 * lax.erf(values * math.sqrt(0.5))
    density = jnp.exp(-0.5 * values * values) * (1.0 / math.sqrt(2.0 * math.pi))
    return values * phi, phi + values * density


def norm_back(grad, normal, scale):
    mean = jnp.mean(grad, axis=-1, keepdims=True)
    along = jnp.mean(grad * normal, axis=-1, keepdims=True)
    return scale * (grad - mean - normal * along)


def fold(values):
    rows, width = values.shape
    return jnp.sum(values.reshape(rows // 8, 8, width), axis=0)


def dot(left, right):
    return jnp.dot(left, right, preferred_element_type=f32)


def dot_rows(left, right):
    return lax.dot_general(left, right, (((0,), (0,)), ((), ())), preferred_element_type=f32)


def dot_cols(left, right):
    return lax.dot_general(left, right, (((1,), (1,)), ((), ())), preferred_element_type=f32)


class Row:
    def __init__(self, ref):
        self.ref = ref

    def __getitem__(self, _):
        return self.ref[...].reshape(1, -1)


class Place:
    def __init__(self, rows, seq):
        self.rows, self.seq = rows, seq
        self.r, self.s = lax.axis_index("rows"), lax.axis_index("seq")
        self.size = sizes_of(rows, seq)
        z = lax.div(self.r, 2)
        self.at = {
            "c": lax.rem(self.s, 2),
            "x": lax.div(self.s, 2),
            "y": lax.rem(self.r, 2),
            "z": z,
            "p": lax.rem(z, 2),
            "q": lax.div(z, 2),
        }

    def peer(self, dim, index):
        at = dict(self.at)
        at[dim] = index
        z = at["q"] * 2 + at["p"] if dim in "pq" else at["z"]
        return (z * 2 + at["y"], at["x"] * 2 + at["c"])


def sizes_of(rows, seq):
    return {"c": 2, "x": seq // 2, "y": 2, "z": rows // 2, "p": 2, "q": rows // 4}


def split(index):
    if isinstance(index, int):
        return index // 2, index % 2
    return lax.div(index, 2), lax.rem(index, 2)


class Reduction:
    def __init__(self, place, order, send, got, send_sem, recv_sem):
        self.place, self.order = place, "c" + order
        self.send, self.got, self.send_sem, self.recv_sem = send, got, send_sem, recv_sem
        self.at = [place.at[d] for d in self.order]
        self.size = [place.size[d] for d in self.order]

    def index(self, r, s):
        z, y = split(r)
        q, p = split(z)
        where = {"c": s % 2, "x": s // 2, "y": y, "z": z, "p": p, "q": q}
        return tuple(where[d] for d in self.order)

    def copies(self, stage):
        n, at = self.size[stage], self.at[stage]
        base = sum(self.size[:stage]) - stage
        found = []
        for off in range(1, n):
            other = lax.rem(at + off, n)
            slot = n - 1 - off
            found.append(
                (
                    other,
                    functools.partial(
                        pltpu.make_async_remote_copy,
                        src_ref=self.send.at[tuple(self.at[:stage]) + (other,)],
                        dst_ref=self.got[stage].at[slot],
                        send_sem=self.send_sem.at[slot],
                        recv_sem=self.recv_sem.at[base + slot],
                        device_id=self.place.peer(self.order[stage], other),
                        device_id_type=MESH,
                    ),
                )
            )
        return found

    def total(self, stage, prefix, rest):
        value = self.send[tuple(prefix) + rest].astype(f32)
        for s in range(stage):
            for slot in range(self.size[s] - 1):
                value = value + self.got[s][(slot,) + tuple(prefix[s + 1 :]) + rest].astype(f32)
        return value

    def start(self):
        for _, copy in self.copies(0):
            copy().start()

    def step(self, stage):
        for _, copy in self.copies(stage - 1):
            copy().wait()
        for other, copy in self.copies(stage):
            prefix = self.at[:stage] + [other]
            lead = self.size[stage + 1 :]
            if not lead:
                self.send[tuple(prefix)] = self.total(stage, prefix, ()).astype(bf16)
            else:
                count = math.prod(lead)

                def add(i, carry, prefix=prefix, lead=lead):
                    rest = []
                    for n in reversed(lead):
                        rest.insert(0, lax.rem(i, n))
                        i = lax.div(i, n)
                    rest = tuple(rest)
                    self.send[tuple(prefix) + rest] = self.total(stage, prefix, rest).astype(bf16)
                    return carry

                lax.fori_loop(0, count, add, 0)
            copy().start()

    def finish(self):
        last = len(self.order) - 1
        for _, copy in self.copies(last):
            copy().wait()
        return self.total(last + 1, self.at, ())


JOBS = {
    "up": ("pxyq", (("up", 0, 0, 10),)),
    "conv0": ("yxz", (("conv", 0, 0, 8),)),
    "conv1": ("xyz", (("conv", 0, 8, 10), ("conv", 1, 0, 6))),
    "conv2": ("ypxq", (("conv", 1, 6, 10), ("conv", 2, 0, 4))),
    "conv3": ("yxz", (("conv", 2, 4, 10),)),
    "conv4": ("pxyq", (("conv", 3, 0, 8),)),
    "conv5": ("xypq", (("conv", 3, 8, 10), ("conv", 4, 0, 4))),
    "conv6": ("yxpq", (("conv", 4, 4, 10),)),
    "down0": ("ypxq", (("down", 0, 0, 4),)),
    "down1": ("pyxq", (("down", 0, 4, 7),)),
    "down2": ("xypq", (("down", 0, 7, 10),)),
}


SCHEDULE = {
    "conv": (("up", 1), ("conv0", 1), ("conv1", 1),),
    "back0": (("conv2", 1),),
    "back1": (("conv3", 1), ("conv4", 1), ("conv5", 1), ("conv6", 1),),
    "back2": (("conv0", 2),),
    "back3": (("conv1", 2),),
    "down": (("conv2", 2), ("conv5", 2), ("up", 2),),
    "first0": (("conv0", 3), ("early", 1), ("conv3", 2),),
    "first1": (("down0", 1), ("down1", 1), ("down2", 1),),
    "first2": (("conv4", 2), ("conv6", 2),),
    "first3": (("conv2", 3), ("conv1", 3),),
    "output0": (("conv5", 3), ("conv0", 4),),
    "output1": (("up", 3), ("early", 2),),
    "end": (("conv3", 3), ("down1", 2), ("down0", 2), ("down2", 2), ("conv1", 4), ("conv5", 4), ("up", 4), ("conv4", 3), ("conv3", 4), ("down1", 3), ("conv6", 3), ("late", 1), ("down0", 3), ("conv2", 4), ("down2", 3), ("conv5", 5), ("early", 3), ("conv4", 4), ("down1", 4), ("conv6", 4), ("up", 5), ("down0", 4), ("late", 2), ("conv2", 5), ("down2", 4), ("conv4", 5), ("down1", 5), ("late", 3), ("conv6", 5), ("down0", 5), ("down2", 5),),
}


class Sizes:
    def __init__(self, rows, seq, micro, length, width, inner, taps):
        self.rows, self.seq = rows, seq
        self.micro, self.length, self.width, self.inner, self.taps = micro, length, width, inner, taps
        self.positions = micro * length
        self.margin = taps // 2 * DILATION
        assert self.margin <= length
        self.share = {
            "up": (inner // rows, width // seq),
            "conv": (inner // rows, inner // seq),
            "down": (inner // seq, width // rows),
        }
        self.unroll = rows * seq <= 32
        assert width == 2 * inner and micro % 2 == 0 and micro // 2 * length <= inner and taps == 5

    def groups(self, matrix, begin, end):
        count = up_to(self.share[matrix][0], 16) // 16
        return range(count * begin // 10, count * end // 10)

    def lanes(self, name):
        found, lane = [], 0
        for matrix, tap, begin, end in JOBS[name][1]:
            for group in self.groups(matrix, begin, end):
                found.append((matrix, tap, group, lane))
                lane += self.share[matrix][1]
        return found, lane

    def block(self, name):
        return (16, up_to(self.lanes(name)[1], 128))


def micro_loads(z):
    return z.micro + 5


def kernel(sizes, *refs):
    (
        x_hbm, seg, c_hbm, n1g, n1s, wd_hbm, db, n2g, n2s, wc_hbm, cb, n3g, n3s, wu_hbm, ub,
        x, c, vec_out, down_out, conv_out, up_out,
        wd, wc, wu, first, slope1, stat1, normal2, scale2, slope2, sext, gext, masks,
        third, masked, held, product, own_labels, labels,
        down_turned, sum1, sum2,
        own_early, got_early, part_early, far_early, total_early, own_late, got_late, part_late, far_late, total_late,
        load_sem, halo_send, halo_recv, label_send, label_recv, *rest,
    ) = refs
    z = sizes
    vectors, (vec_send, vec_recv), job_refs = rest[:9], rest[9:11], rest[11:]
    vector_refs = (
        own_early, got_early, part_early, far_early, total_early, own_late, got_late, part_late, far_late, total_late,
    )
    in_hbm = (n1g, n1s, db, n2g, n2s, cb, n3g, n3s, ub)
    vector_loads = [
        pltpu.make_async_copy(source, target, load_sem.at[micro_loads(z) + k])
        for k, (source, target) in enumerate(zip(in_hbm, vectors))
    ]
    n1g, n1s, db, n2g, n2s, cb, n3g, n3s, ub = (Row(ref) for ref in vectors)
    micro, length, width, inner, taps = z.micro, z.length, z.width, z.inner, z.taps
    place = Place(z.rows, z.seq)
    me_r, me_s = place.r, place.s
    has_left, has_right = me_s > 0, me_s < z.seq - 1
    left = (me_r, jnp.maximum(me_s - 1, 0))
    right = (me_r, jnp.minimum(me_s + 1, z.seq - 1))
    jobs = {}
    for name, (order, _) in JOBS.items():
        send, *got, send_sem, recv_sem = job_refs[: len(order) + 4]
        job_refs = job_refs[len(order) + 4 :]
        jobs[name] = Reduction(place, order, send, got, send_sem, recv_sem)

    def start_reductions(*sources):
        for name, (_, parts) in JOBS.items():
            matrix, tap, _, _ = parts[-1]
            if (tap if matrix == "conv" else matrix) in sources:
                jobs[name].start()

    def steps(phase):
        for name, stage in SCHEDULE.get(phase, ()):
            if name in ("early", "late"):
                vector_step(("early", "late").index(name), stage)
            elif stage < len(jobs[name].order):
                jobs[name].step(stage)
            else:
                finish(name)

    def steps_in(phase, count, i):
        for k in range(count):
            if SCHEDULE.get(phase + str(k)):

                @pl.when(i == k)
                def _(k=k):
                    steps(phase + str(k))

    def load_x(i):
        return pltpu.make_async_copy(x_hbm.at[i], x.at[i], load_sem.at[i])

    weight_loads = [
        pltpu.make_async_copy(source, target, load_sem.at[micro + k])
        for k, (source, target) in enumerate(
            ((wd_hbm, wd), (wu_hbm, wu), (wc_hbm, wc), (c_hbm, c), (seg, own_labels.at[pl.ds(0, micro)]))
        )
    ]
    load_x(0).start()
    for copy in vector_loads:
        copy.start()
    weight_loads[0].start()
    for i in range(1, micro):
        load_x(i).start()
    for k in (4, 3, 1, 2):
        weight_loads[k].start()

    barrier = pltpu.get_barrier_semaphore()
    for off in range(1, z.seq):
        pl.semaphore_signal(
            barrier, inc=1, device_id=(me_r, lax.rem(me_s + off, z.seq)), device_id_type=MESH
        )
    for off in range(1, z.rows):
        pl.semaphore_signal(
            barrier, inc=1, device_id=(lax.rem(me_r + off, z.rows), me_s), device_id_type=MESH
        )

    own_labels[micro:, :] = jnp.zeros((own_labels.shape[0] - micro, length), jnp.int32)
    sum1[...] = jnp.zeros(sum1.shape, f32)
    sum2[...] = jnp.zeros(sum2.shape, f32)

    @pl.when(jnp.logical_not(has_left))
    def _():
        labels[0] = jnp.full(labels.shape[1:], -1, jnp.int32)
        sext[:, 0:length, :] = jnp.zeros((micro, length, inner), bf16)
        gext[:, 0:length, :] = jnp.zeros((micro, length, inner), bf16)

    @pl.when(jnp.logical_not(has_right))
    def _():
        labels[1] = jnp.full(labels.shape[1:], -1, jnp.int32)
        sext[:, 2 * length :, :] = jnp.zeros((micro, length, inner), bf16)
        gext[:, 2 * length :, :] = jnp.zeros((micro, length, inner), bf16)

    def halo(ext, turn, i):
        return (
            (
                has_right,
                pltpu.make_async_remote_copy(
                    src_ref=ext.at[i, pl.ds(length, length)],
                    dst_ref=ext.at[i, pl.ds(0, length)],
                    send_sem=halo_send.at[0, i],
                    recv_sem=halo_recv.at[turn, 0, i],
                    device_id=right,
                    device_id_type=MESH,
                ),
            ),
            (
                has_left,
                pltpu.make_async_remote_copy(
                    src_ref=ext.at[i, pl.ds(length, length)],
                    dst_ref=ext.at[i, pl.ds(2 * length, length)],
                    send_sem=halo_send.at[1, i],
                    recv_sem=halo_recv.at[turn, 1, i],
                    device_id=left,
                    device_id_type=MESH,
                ),
            ),
        )

    def label_copies():
        return [
            (
                ok,
                pltpu.make_async_remote_copy(
                    src_ref=own_labels,
                    dst_ref=labels.at[way],
                    send_sem=label_send.at[way],
                    recv_sem=label_recv.at[way],
                    device_id=target,
                    device_id_type=MESH,
                ),
            )
            for way, (ok, target) in enumerate(((has_right, right), (has_left, left)))
        ]

    def start_all(copies):
        for ok, copy in copies:
            pl.when(ok)(copy.start)

    def wait_sent(copies):
        for ok, copy in copies:
            pl.when(ok)(copy.wait_send)

    def wait_got(copies):
        pl.when(has_left)(copies[0][1].wait_recv)
        pl.when(has_right)(copies[1][1].wait_recv)

    def first_half(i):
        chunk = min(128, length)
        for begin in range(0, length, chunk):
            some = pl.ds(begin, chunk)
            mean, scale, normal = normalise(x[i, some, :].astype(f32))
            act, slope = gelu_and_slope(normal * n1g[...] + n1s[...])
            first[i, some, :] = act.astype(bf16)
            slope1[i, some, :] = slope.astype(bf16)
            stat1[0, i, some, :] = jnp.broadcast_to(mean, (chunk, 128))
            stat1[1, i, some, :] = jnp.broadcast_to(scale, (chunk, 128))

    def second_half(i, reduced):
        _, scale, normal = normalise(reduced)
        act, slope = gelu_and_slope(normal * n2g[...] + n2s[...])
        sext[i, pl.ds(length, length), :] = act.astype(bf16)
        slope2[i] = slope.astype(bf16)
        normal2[i] = normal.astype(bf16)
        scale2[i] = jnp.broadcast_to(scale, (length, 128))

    def repeat(count, body):
        if z.unroll:
            for i in range(count):
                body(i)
        else:
            lax.fori_loop(0, count, lambda i, carry: (body(i), carry)[1], 0)

    for name, job in jobs.items():
        used, lanes = z.lanes(name)[1], job.send.shape[-1]
        if used < lanes:
            job.send[..., used:] = jnp.zeros(job.send.shape[:-1] + (lanes - used,), bf16)
    load_x(0).wait()
    for copy in vector_loads:
        copy.wait()
    first_half(0)
    weight_loads[0].wait()

    def head(i, carry):
        load_x(i + 1).wait()
        reduced = dot(first[i], wd[...]) + db[...]
        first_half(i + 1)
        second_half(i, reduced)

        @pl.when(i == 0)
        def _():
            weight_loads[4].wait()
            pl.semaphore_wait(barrier, z.seq + z.rows - 2)
            start_all(label_copies())

        start_all(halo(sext, 0, i))
        return carry

    lax.fori_loop(0, micro - 1, head, 0)

    def third_grad_at(i):
        row, column = split(i)
        if isinstance(i, int):
            return pl.ds(row * length, length), pl.ds(column * inner, inner)
        return (
            pl.ds(pl.multiple_of(row * length, 128), length),
            pl.ds(pl.multiple_of(column * inner, 128), inner),
        )

    weight_loads[1].wait()
    weight_loads[3].wait()
    reduced = dot(first[micro - 1], wd[...]) + db[...]
    for i in range(0, micro, 2):
        grads = dot_cols(c[i : i + 2].reshape(2 * length, width), wu[...])
        for j in range(2):
            product[third_grad_at(i + j)] = grads[j * length : (j + 1) * length]
            sum1[0] += fold(c[i + j].astype(f32))
    second_half(micro - 1, reduced)
    start_all(halo(sext, 0, micro - 1))

    weight_loads[2].wait()
    wait_got(label_copies())
    wait_got(halo(sext, 0, 0))
    spread = jnp.concatenate([labels[0], own_labels[...], labels[1]], axis=1).astype(f32).T
    for i in range(micro):
        column = spread[:, i : i + 1]
        centre = column[length : 2 * length]
        for n, k in enumerate(k for k in range(taps) if k != taps // 2):
            begin = length - z.margin + k * DILATION
            same = (column[begin : begin + length] == centre).astype(f32)
            masks[n, i] = jnp.broadcast_to(same, (length, 128)).astype(bf16)

    def tap_of(ext, i, k):
        begin = length - z.margin + k * DILATION
        block = ext[i, pl.ds(begin, length), :]
        if k == taps // 2:
            return block
        keep = masks[k if k < taps // 2 else k - 1, i]
        return block * jnp.concatenate([keep] * (inner // 128), axis=1)

    def convolve(i, beside=lambda part: None):
        conv = cb[...]
        for k in range(taps):
            conv = conv + dot(tap_of(sext, i, k), wc[k])
            beside(k)
        return conv.astype(bf16)

    parts = [pl.ds(begin, length // 4) for begin in range(0, length, length // 4)]

    def middle(i, part):
        if part >= len(parts):
            return
        some = parts[part]
        mixed = held[some, :].astype(f32)
        _, scale, normal = normalise(mixed)
        act, slope = gelu_and_slope(normal * n3g[...] + n3s[...])
        third[i, some, :] = act.astype(bf16)
        row, column = third_grad_at(i)
        grad = product[pl.ds(row.start + some.start, some.size), column] * slope
        sum2[0] += fold(grad * normal)
        sum2[1] += fold(grad)
        mixed_grad = norm_back(grad * n3g[...], normal, scale).astype(bf16)
        gext[i, pl.ds(length + some.start, some.size), :] = mixed_grad
        sum2[2] += fold(mixed_grad.astype(f32))

    held[...] = convolve(0)

    def middle_step(i, carry):
        wait_got(halo(sext, 0, i + 1))
        held[...] = convolve(i + 1, lambda part: middle(i, part))
        wait_sent(halo(sext, 0, i))
        start_all(halo(gext, 1, i))
        return carry

    lax.fori_loop(0, micro - 1, middle_step, 0)
    for part in range(len(parts)):
        middle(micro - 1, part)
    wait_sent(halo(sext, 0, micro - 1))
    start_all(halo(gext, 1, micro - 1))

    def finish(name):
        value = jobs[name].finish()
        for matrix, tap, group, lane in z.lanes(name)[0]:
            rows, columns = z.share[matrix]
            target = {"up": up_out, "conv": conv_out.at[tap], "down": down_turned}[matrix]
            count = min(16, rows - 16 * group)
            target[pl.ds(16 * group, count), :] = value[:count, lane : lane + columns]

    whole = lambda ref: ref[...].reshape(z.positions, ref.shape[-1])
    own = lambda ext: ext[:, length : 2 * length, :].reshape(z.positions, inner)

    def pack(matrix, tap, base, rows_over):
        share = z.share[matrix]
        over_rows, over_columns = (z.rows, z.seq) if rows_over == "rows" else (z.seq, z.rows)
        targets = [
            (job, group, lane)
            for name, job in jobs.items()
            for m, t, group, lane in z.lanes(name)[0]
            if (m, t) == (matrix, tap)
        ]

        def pack_rows(k):
            begin = k * share[0]
            if not isinstance(k, int):
                begin = pl.multiple_of(begin, 8)
            rows = product[pl.ds(begin, share[0]), base : base + over_columns * share[1]]
            for j in range(over_columns):
                piece = rows[:, j * share[1] : (j + 1) * share[1]]
                for job, group, lane in targets:
                    at = job.index(k, j) if rows_over == "rows" else job.index(j, k)
                    some = piece[16 * group : min(16 * group + 16, share[0])]
                    short = 16 - some.shape[0]
                    if short:
                        some = jnp.concatenate([some, jnp.zeros((short, share[1]), f32)], axis=0)
                    job.send[at + (slice(None), pl.ds(lane, share[1]))] = some.astype(bf16)

        repeat(over_rows, pack_rows)

    def conv_weight_grad(k):
        if k == taps // 2:
            source = own(sext)
        else:
            for i in range(micro):
                masked[i] = tap_of(sext, i, k)
            source = whole(masked)
        base = k % 2 * inner
        product[:, base : base + inner] = dot_rows(source, own(gext))
        pack("conv", k, base, "rows")

    product[...] = dot_rows(whole(third), whole(c))
    pack("up", 0, 0, "rows")
    conv_weight_grad(0)
    conv_weight_grad(1)
    start_reductions("up", 0, 1)
    steps("up")
    for k in range(2, taps):
        conv_weight_grad(k)
    start_reductions(*range(2, taps))
    steps("conv")

    def convolve_back(i, beside=lambda part: None):
        grad = dot_cols(tap_of(gext, i, 0), wc[taps - 1])
        beside(0)
        for k in range(1, taps):
            grad = grad + dot_cols(tap_of(gext, i, k), wc[taps - 1 - k])
            beside(k)
        return grad.astype(bf16)

    def second_back(i, part):
        if part >= len(parts):
            return
        some = parts[part]
        grad = held[some, :].astype(f32) * slope2[i, some, :].astype(f32)
        normal = normal2[i, some, :].astype(f32)
        sum2[3] += fold(grad * normal)
        sum2[4] += fold(grad)
        scale = jnp.concatenate([scale2[i, some, :]] * (inner // 128), axis=1)
        reduced_grad = norm_back(grad * n2g[...], normal, scale).astype(bf16)
        sext[i, some, :] = reduced_grad
        sum2[5] += fold(reduced_grad.astype(f32))

    wait_got(halo(gext, 1, 0))
    held[...] = convolve_back(0)
    steps("back0")

    def conv_back_step(i, carry):
        wait_got(halo(gext, 1, i + 1))
        held[...] = convolve_back(i + 1, lambda part: second_back(i, part))

        steps_in("back", micro - 1, i + 1)
        return carry

    lax.fori_loop(0, micro - 1, conv_back_step, 0)
    for part in range(len(parts)):
        second_back(micro - 1, part)
    steps("back3")

    half = width // 2

    group, mine = lax.div(me_s, SLICES) * SLICES, lax.rem(me_s, SLICES)

    def vector_copies(turn, stage):
        own, got, part, far, total = vector_refs[5 * turn : 5 * turn + 5]
        me, count = ((me_s, z.seq), (me_r, z.rows), (mine, SLICES))[stage]
        inbox = (got, far, total)[stage]
        sends = []
        for off in range(1, count):
            other = lax.rem(me + off, count)
            target = ((me_r, other), (other, me_s), (me_r, group + other))[stage]
            source = (own.at[lax.rem(other, SLICES)], part, total.at[mine])[stage]
            sends.append(
                functools.partial(
                    pltpu.make_async_remote_copy,
                    src_ref=source,
                    dst_ref=inbox.at[me],
                    send_sem=vec_send.at[turn, stage],
                    recv_sem=vec_recv.at[turn, stage],
                    device_id=target,
                    device_id_type=MESH,
                )
            )
        return sends, inbox.at[pl.ds(0, count - 1)]

    def vector_start(turn, stage):
        for copy in vector_copies(turn, stage)[0]:
            copy().start()

    def vector_wait(turn, stage, sem):
        some = vector_copies(turn, stage)[1]
        pltpu.make_async_copy(some, some, sem.at[turn, stage]).wait()

    def vector_sent(turn):
        for stage in range(3):
            vector_wait(turn, stage, vec_send)

    def vector_step(turn, stage):
        own, got, part, far, total = vector_refs[5 * turn : 5 * turn + 5]
        vector_wait(turn, stage - 1, vec_recv)
        if stage == 3:
            rows = own.shape[1]
            for k in range(SLICES):
                begin = (0, 8)[turn] + k * rows
                vec_out[begin : begin + rows, :] = total[k]
            vector_sent(turn)
            return
        me, count = ((me_s, z.seq), (me_r, z.rows))[stage - 1]
        inbox = (got, far)[stage - 1]
        inbox[me] = (own[mine], part[...])[stage - 1]
        value = inbox[0]
        for k in range(1, count):
            value = value + inbox[k]
        if stage == 1:
            part[...] = value
        else:
            total[mine] = value
        vector_start(turn, stage)

    def squeeze(value):
        return jnp.sum(value, axis=0, keepdims=True)

    early = [squeeze(sum1[0, :, h * half : (h + 1) * half]) for h in range(2)]
    early += [squeeze(sum2[k]) for k in range(6)]
    for k, row in enumerate(early):
        vector_refs[0][k // 2, k % 2 : k % 2 + 1, :] = row
    vector_start(0, 0)

    reduced_grads = sext[:, 0:length, :].reshape(z.positions, inner)
    product[...] = dot_rows(reduced_grads, whole(first))
    pack("down", 0, 0, "seq")
    start_reductions("down")
    steps("down")

    def first_back(i, carry):
        grads = dot_cols(sext[i, pl.ds(0, length), :], wd[...])
        chunk = min(128, length)
        for begin in range(0, length, chunk):
            some = pl.ds(begin, chunk)
            grad = grads[begin : begin + chunk] * slope1[i, some, :].astype(f32)
            mean = jnp.concatenate([stat1[0, i, some, :]] * (width // 128), axis=1)
            scale = jnp.concatenate([stat1[1, i, some, :]] * (width // 128), axis=1)
            normal = (x[i, some, :].astype(f32) - mean) * scale
            sum1[1] += fold(grad * normal)
            sum1[2] += fold(grad)
            part = norm_back(grad * n1g[...], normal, scale)
            c[i, some, :] = (c[i, some, :].astype(f32) + part).astype(bf16)

        steps_in("first", micro - 1, i)
        return carry

    lax.fori_loop(0, micro, first_back, 0)
    late = [squeeze(sum1[k, :, h * half : (h + 1) * half]) for k in (1, 2) for h in range(2)]
    for k, row in enumerate(late):
        vector_refs[5][k] = row
    vector_start(1, 0)
    steps("first3")

    def finish_output(i, carry):
        x[i] = (x[i].astype(f32) + dot(third[i], wu[...]) + ub[...]).astype(bf16)

        steps_in("output", micro - 1, i)
        return carry

    lax.fori_loop(0, micro, finish_output, 0)
    for i in range(micro):
        wait_sent(halo(gext, 1, i))
    wait_sent(label_copies())
    steps("end")
    down_out[...] = down_turned[...].T


def per_device(z, x, seg, c, n1g, n1s, wd, db, n2g, n2s, wc, cb, n3g, n3s, wu, ub):
    micro, length, width, inner, taps = z.micro, z.length, z.width, z.inner, z.taps
    rows = lambda last, kind: pltpu.VMEM((micro, length, last), kind)
    job_scratch = []
    n = sizes_of(z.rows, z.seq)
    for name, (order, _) in JOBS.items():
        block = z.block(name)
        lead = tuple(n[d] for d in "c" + order)
        job_scratch.append(pltpu.VMEM(lead + block, bf16))
        for stage in range(len(lead)):
            job_scratch.append(pltpu.VMEM((lead[stage] - 1,) + lead[stage + 1 :] + block, bf16))
        job_scratch.append(pltpu.SemaphoreType.DMA((max(lead) - 1,)))
        job_scratch.append(pltpu.SemaphoreType.DMA((sum(lead) - len(lead),)))
    scratch = [
        pltpu.VMEM((width, inner), bf16),
        pltpu.VMEM((taps, inner, inner), bf16),
        pltpu.VMEM((inner, width), bf16),
        rows(width, bf16),
        rows(width, bf16),
        pltpu.VMEM((2, micro, length, 128), f32),
        rows(inner, bf16),
        rows(128, f32),
        rows(inner, bf16),
        pltpu.VMEM((micro, 3 * length, inner), bf16),
        pltpu.VMEM((micro, 3 * length, inner), bf16),
        pltpu.VMEM((taps - 1, micro, length, 128), bf16),
        rows(inner, bf16),
        rows(inner, bf16),
        pltpu.VMEM((length, inner), bf16),
        pltpu.VMEM((inner, width), f32),
        pltpu.VMEM((8, length), jnp.int32),
        pltpu.VMEM((2, 8, length), jnp.int32),
        pltpu.VMEM(z.share["down"], f32),
        pltpu.VMEM((3, 8, width), f32),
        pltpu.VMEM((6, 8, inner), f32),
    ] + [
        pltpu.VMEM(lead + (rows_of, inner), f32)
        for rows_of in (2, 1)
        for lead in ((SLICES,), (z.seq,), (), (z.rows,), (SLICES,))
    ] + [
        pltpu.SemaphoreType.DMA((micro_loads(z) + 9,)),
        pltpu.SemaphoreType.DMA((2, micro)),
        pltpu.SemaphoreType.DMA((2, 2, micro)),
        pltpu.SemaphoreType.DMA((2,)),
        pltpu.SemaphoreType.DMA((2,)),
    ] + [
        pltpu.VMEM(v.shape, f32) for v in (n1g, n1s, db, n2g, n2s, cb, n3g, n3s, ub)
    ] + [
        pltpu.SemaphoreType.DMA((2, 3))
        for _ in range(2)
    ] + job_scratch
    out, ig, vectors, down, conv, up = pl.pallas_call(
        functools.partial(kernel, z),
        out_shape=(
            pltpu.VMEM(x.shape, bf16),
            pltpu.VMEM(x.shape, bf16),
            pltpu.VMEM((16, inner), f32),
            pltpu.VMEM(z.share["down"][::-1], f32),
            pltpu.VMEM((taps,) + z.share["conv"], f32),
            pltpu.VMEM(z.share["up"], f32),
        ),
        in_specs=[ANY] * 15,
        out_specs=(VMEM,) * 6,
        scratch_shapes=scratch,
        compiler_params=pltpu.CompilerParams(
            collective_id=0, has_side_effects=True, vmem_limit_bytes=58 << 20
        ),
    )(
        x, seg, c, n1g, n1s, wd, db, n2g, n2s, wc, cb, n3g, n3s, wu, ub,
    )
    vector = lambda n: jax.ShapeDtypeStruct((n,), f32)
    out, ig, down, conv, up, *vectors = pl.pallas_call(
        write_out,
        out_shape=(
            jax.ShapeDtypeStruct(x.shape, bf16),
            jax.ShapeDtypeStruct(x.shape, bf16),
            jax.ShapeDtypeStruct(z.share["down"][::-1], f32),
            jax.ShapeDtypeStruct((taps,) + z.share["conv"], f32),
            jax.ShapeDtypeStruct(z.share["up"], f32),
        )
        + tuple(vector(width if first + 1 < last else inner) for first, last in VECTORS),
        in_specs=[VMEM] * 6,
        out_specs=(ANY,) * (5 + len(VECTORS)),
        scratch_shapes=[pltpu.VMEM((width if first + 1 < last else inner,), f32) for first, last in VECTORS]
        + [pltpu.SemaphoreType.DMA((5 + len(VECTORS),))],
        compiler_params=pltpu.CompilerParams(vmem_limit_bytes=2 << 20),
    )(*(pltpu.with_memory_space_constraint(v, pltpu.VMEM) for v in (out, ig, vectors, down, conv, up)))
    ub, n3g, n3s, cb, n2g, n2s, db, n1g, n1s = vectors
    return out, ig, n1g, n1s, down, db, n2g, n2s, conv, cb, n3g, n3s, up, ub


VECTORS = ((0, 2), (2, 3), (3, 4), (4, 5), (5, 6), (6, 7), (7, 8), (8, 10), (10, 12))


def write_out(out, ig, vectors, down, conv, up, *rest):
    count = len(VECTORS)
    targets, rows, sem = rest[: 5 + count], rest[5 + count : -1], rest[-1]
    width = vectors.shape[1]
    sources = (out, ig, down, conv, up) + rows
    copies = [
        pltpu.make_async_copy(source, target, sem.at[k])
        for k, (source, target) in enumerate(zip(sources, targets))
    ]
    for copy in copies[:5]:
        copy.start()
    for row, (begin, end) in zip(rows, VECTORS):
        for k in range(begin, end):
            row[pl.ds((k - begin) * width, width)] = vectors[k, :]
    for copy in copies[5:]:
        copy.start()
    for copy in copies:
        copy.wait()


def solution(mesh):
    def step(*args):
        micro, length, width = args[0].shape
        taps, inner, _ = args[9].shape
        z = Sizes(mesh.shape["rows"], mesh.shape["seq"], micro, length, width, inner, taps)
        return per_device(z, *args)

    rows = P("rows", "seq", None)
    matrix = P("rows", "seq")
    return jax.shard_map(
        step,
        mesh=mesh,
        in_specs=(rows, matrix, rows) + (P(),) * 12,
        out_specs=(rows, rows, P(), P(), matrix, P(), P(), P(), P(None, "rows", "seq"))
        + (P(),) * 3
        + (matrix, P()),
        check_vma=False,
    )
```

```python
import functools
import math

import jax
import jax.numpy as jnp
from jax import lax
from jax.experimental import pallas as pl
from jax.experimental.pallas import tpu as pltpu
from jax.sharding import PartitionSpec as P

DILATION = 128
EPSILON = 1e-05
MESH = pl.DeviceIdType.MESH
SLICES = 4
bf16 = jnp.bfloat16
f32 = jnp.float32
ANY = pl.BlockSpec(memory_space=pl.ANY)
VMEM = pl.BlockSpec(memory_space=pltpu.VMEM)


def up_to(value, step):
    return -(-value // step) * step


def normalise(values):
    mean = jnp.mean(values, axis=-1, keepdims=True)
    centred = values - mean
    scale = lax.rsqrt(jnp.mean(centred * centred, axis=-1, keepdims=True) + EPSILON)
    return mean, scale, centred * scale


def gelu_and_slope(values):
    phi = 0.5 + 0.5 * lax.erf(values * math.sqrt(0.5))
    density = jnp.exp(-0.5 * values * values) * (1.0 / math.sqrt(2.0 * math.pi))
    return values * phi, phi + values * density


def norm_back(grad, normal, scale):
    mean = jnp.mean(grad, axis=-1, keepdims=True)
    along = jnp.mean(grad * normal, axis=-1, keepdims=True)
    return scale * (grad - mean - normal * along)


def fold(values):
    rows, width = values.shape
    return jnp.sum(values.reshape(rows // 8, 8, width), axis=0)


def dot(left, right):
    return jnp.dot(left, right, preferred_element_type=f32)


def dot_rows(left, right):
    return lax.dot_general(left, right, (((0,), (0,)), ((), ())), preferred_element_type=f32)


def dot_cols(left, right):
    return lax.dot_general(left, right, (((1,), (1,)), ((), ())), preferred_element_type=f32)


class Row:
    def __init__(self, ref):
        self.ref = ref

    def __getitem__(self, _):
        return self.ref[...].reshape(1, -1)


class Place:
    def __init__(self, rows, seq):
        self.rows, self.seq = rows, seq
        self.r, self.s = lax.axis_index("rows"), lax.axis_index("seq")
        self.size = sizes_of(rows, seq)
        z = lax.div(self.r, 2)
        self.at = {
            "c": lax.rem(self.s, 2),
            "x": lax.div(self.s, 2),
            "y": lax.rem(self.r, 2),
            "z": z,
            "p": lax.rem(z, 2),
            "q": lax.div(z, 2),
        }

    def peer(self, dim, index):
        at = dict(self.at)
        at[dim] = index
        z = at["q"] * 2 + at["p"] if dim in "pq" else at["z"]
        return (z * 2 + at["y"], at["x"] * 2 + at["c"])


def sizes_of(rows, seq):
    return {"c": 2, "x": seq // 2, "y": 2, "z": rows // 2, "p": 2, "q": rows // 4}


def split(index):
    if isinstance(index, int):
        return index // 2, index % 2
    return lax.div(index, 2), lax.rem(index, 2)


class Reduction:
    def __init__(self, place, order, send, got, send_sem, recv_sem):
        self.place, self.order = place, "c" + order
        self.send, self.got, self.send_sem, self.recv_sem = send, got, send_sem, recv_sem
        self.at = [place.at[d] for d in self.order]
        self.size = [place.size[d] for d in self.order]

    def index(self, r, s):
        z, y = split(r)
        q, p = split(z)
        where = {"c": s % 2, "x": s // 2, "y": y, "z": z, "p": p, "q": q}
        return tuple(where[d] for d in self.order)

    def copies(self, stage):
        n, at = self.size[stage], self.at[stage]
        base = sum(self.size[:stage]) - stage
        found = []
        for off in range(1, n):
            other = lax.rem(at + off, n)
            slot = n - 1 - off
            found.append(
                (
                    other,
                    functools.partial(
                        pltpu.make_async_remote_copy,
                        src_ref=self.send.at[tuple(self.at[:stage]) + (other,)],
                        dst_ref=self.got[stage].at[slot],
                        send_sem=self.send_sem.at[slot],
                        recv_sem=self.recv_sem.at[base + slot],
                        device_id=self.place.peer(self.order[stage], other),
                        device_id_type=MESH,
                    ),
                )
            )
        return found

    def total(self, stage, prefix, rest):
        value = self.send[tuple(prefix) + rest].astype(f32)
        for s in range(stage):
            for slot in range(self.size[s] - 1):
                value = value + self.got[s][(slot,) + tuple(prefix[s + 1 :]) + rest].astype(f32)
        return value

    def start(self):
        for _, copy in self.copies(0):
            copy().start()

    def step(self, stage):
        for _, copy in self.copies(stage - 1):
            copy().wait()
        for other, copy in self.copies(stage):
            prefix = self.at[:stage] + [other]
            lead = self.size[stage + 1 :]
            if not lead:
                self.send[tuple(prefix)] = self.total(stage, prefix, ()).astype(bf16)
            else:
                count = math.prod(lead)

                def add(i, carry, prefix=prefix, lead=lead):
                    rest = []
                    for n in reversed(lead):
                        rest.insert(0, i % n if isinstance(i, int) else lax.rem(i, n))
                        i = i // n if isinstance(i, int) else lax.div(i, n)
                    rest = tuple(rest)
                    self.send[tuple(prefix) + rest] = self.total(stage, prefix, rest).astype(bf16)
                    return carry

                if count <= 8:
                    for i in range(count):
                        add(i, 0)
                else:
                    lax.fori_loop(0, count, add, 0)
            copy().start()

    def finish(self):
        last = len(self.order) - 1
        for _, copy in self.copies(last):
            copy().wait()
        return self.total(last + 1, self.at, ())


JOBS = {
    "up": ("pxyq", (("up", 0, 0, 10),)),
    "conv0": ("yxz", (("conv", 0, 0, 8),)),
    "conv1": ("xyz", (("conv", 0, 8, 10), ("conv", 1, 0, 6))),
    "conv2": ("ypxq", (("conv", 1, 6, 10), ("conv", 2, 0, 4))),
    "conv3": ("yxz", (("conv", 2, 4, 10),)),
    "conv4": ("pxyq", (("conv", 3, 0, 8),)),
    "conv5": ("xypq", (("conv", 3, 8, 10), ("conv", 4, 0, 4))),
    "conv6": ("yxpq", (("conv", 4, 4, 10),)),
    "down0": ("ypxq", (("down", 0, 0, 4),)),
    "down1": ("pyxq", (("down", 0, 4, 7),)),
    "down2": ("xypq", (("down", 0, 7, 10),)),
}


SCHEDULE = {
    "conv": (("up", 1), ("conv0", 1), ("conv1", 1),),
    "back0": (("conv2", 1),),
    "back1": (("conv3", 1), ("conv4", 1), ("conv5", 1), ("conv6", 1),),
    "back2": (("conv0", 2),),
    "back3": (("conv1", 2),),
    "down": (("conv2", 2), ("conv5", 2), ("up", 2),),
    "first0": (("conv0", 3), ("early", 1), ("conv3", 2),),
    "first1": (("down0", 1), ("down1", 1), ("down2", 1),),
    "first2": (("conv4", 2), ("conv6", 2),),
    "first3": (("conv2", 3), ("conv1", 3),),
    "output0": (("conv5", 3), ("conv0", 4),),
    "output1": (("up", 3), ("early", 2),),
    "end": (("conv3", 3), ("down1", 2), ("down0", 2), ("down2", 2), ("conv1", 4), ("conv5", 4), ("up", 4), ("conv4", 3), ("conv3", 4), ("down1", 3), ("conv6", 3), ("late", 1), ("down0", 3), ("conv2", 4), ("down2", 3), ("conv5", 5), ("early", 3), ("conv4", 4), ("down1", 4), ("conv6", 4), ("up", 5), ("down0", 4), ("late", 2), ("conv2", 5), ("down2", 4), ("conv4", 5), ("down1", 5), ("late", 3), ("conv6", 5), ("down0", 5), ("down2", 5),),
}


class Sizes:
    def __init__(self, rows, seq, micro, length, width, inner, taps):
        self.rows, self.seq = rows, seq
        self.micro, self.length, self.width, self.inner, self.taps = micro, length, width, inner, taps
        self.positions = micro * length
        self.margin = taps // 2 * DILATION
        assert self.margin <= length
        self.share = {
            "up": (inner // rows, width // seq),
            "conv": (inner // rows, inner // seq),
            "down": (inner // seq, width // rows),
        }
        self.unroll = rows * seq <= 32
        assert width == 2 * inner and micro % 2 == 0 and micro >= taps - 1 and micro // 2 * length <= inner and taps == 5

    def groups(self, matrix, begin, end):
        count = up_to(self.share[matrix][0], 16) // 16
        return range(count * begin // 10, count * end // 10)

    def lanes(self, name):
        found, lane = [], 0
        for matrix, tap, begin, end in JOBS[name][1]:
            for group in self.groups(matrix, begin, end):
                found.append((matrix, tap, group, lane))
                lane += self.share[matrix][1]
        return found, lane

    def block(self, name):
        return (16, up_to(self.lanes(name)[1], 128))


def micro_loads(z):
    return z.micro + 5


def kernel(sizes, *refs):
    (
        x_hbm, seg, c_hbm, n1g, n1s, wd_hbm, db, n2g, n2s, wc_hbm, cb, n3g, n3s, wu_hbm, ub,
        x, c, vec_out, down_out, conv_out, up_out,
        wd, wc, wu, first, slope1, stat1, normal2, scale2, slope2, sext, gext, masks,
        third, masked, held, product, own_labels, labels,
        down_turned, sum1, sum2,
        own_early, got_early, part_early, far_early, total_early, own_late, got_late, part_late, far_late, total_late,
        load_sem, halo_send, halo_recv, label_send, label_recv, *rest,
    ) = refs
    z = sizes
    vectors, (vec_send, vec_recv), job_refs = rest[:9], rest[9:11], rest[11:]
    vector_refs = (
        own_early, got_early, part_early, far_early, total_early, own_late, got_late, part_late, far_late, total_late,
    )
    in_hbm = (n1g, n1s, db, n2g, n2s, cb, n3g, n3s, ub)
    vector_loads = [
        pltpu.make_async_copy(source, target, load_sem.at[micro_loads(z) + k])
        for k, (source, target) in enumerate(zip(in_hbm, vectors))
    ]
    n1g, n1s, db, n2g, n2s, cb, n3g, n3s, ub = (Row(ref) for ref in vectors)
    micro, length, width, inner, taps = z.micro, z.length, z.width, z.inner, z.taps
    place = Place(z.rows, z.seq)
    me_r, me_s = place.r, place.s
    has_left, has_right = me_s > 0, me_s < z.seq - 1
    left = (me_r, jnp.maximum(me_s - 1, 0))
    right = (me_r, jnp.minimum(me_s + 1, z.seq - 1))
    jobs = {}
    for name, (order, _) in JOBS.items():
        send, *got, send_sem, recv_sem = job_refs[: len(order) + 4]
        job_refs = job_refs[len(order) + 4 :]
        jobs[name] = Reduction(place, order, send, got, send_sem, recv_sem)

    def start_reductions(*sources):
        for name, (_, parts) in JOBS.items():
            matrix, tap, _, _ = parts[-1]
            if (tap if matrix == "conv" else matrix) in sources:
                jobs[name].start()

    def steps(phase):
        for name, stage in SCHEDULE.get(phase, ()):
            if name in ("early", "late"):
                vector_step(("early", "late").index(name), stage)
            elif stage < len(jobs[name].order):
                jobs[name].step(stage)
            else:
                finish(name)

    def steps_in(phase, count, i):
        for k in range(count):
            if SCHEDULE.get(phase + str(k)):

                @pl.when(i == k)
                def _(k=k):
                    steps(phase + str(k))

    def load_x(i):
        return pltpu.make_async_copy(x_hbm.at[i], x.at[i], load_sem.at[i])

    weight_loads = [
        pltpu.make_async_copy(source, target, load_sem.at[micro + k])
        for k, (source, target) in enumerate(
            ((wd_hbm, wd), (wu_hbm, wu), (wc_hbm, wc), (c_hbm, c), (seg, own_labels.at[pl.ds(0, micro)]))
        )
    ]
    first_chunks = [
        pltpu.make_async_copy(x_hbm.at[0, some], x.at[0, some], load_sem.at[sem])
        for some, sem in ((pl.ds(0, length // 2), 0), (pl.ds(length // 2, length // 2), micro + 5 + 9))
    ]
    first_chunks[0].start()
    for copy in vector_loads[:2]:
        copy.start()
    first_chunks[1].start()
    for copy in vector_loads[2:]:
        copy.start()
    weight_loads[0].start()
    for i in range(1, micro):
        load_x(i).start()
    for k in (4, 3, 1, 2):
        weight_loads[k].start()

    barrier = pltpu.get_barrier_semaphore()
    for off in range(1, z.seq):
        pl.semaphore_signal(
            barrier, inc=1, device_id=(me_r, lax.rem(me_s + off, z.seq)), device_id_type=MESH
        )
    for off in range(1, z.rows):
        pl.semaphore_signal(
            barrier, inc=1, device_id=(lax.rem(me_r + off, z.rows), me_s), device_id_type=MESH
        )

    own_labels[micro:, :] = jnp.zeros((own_labels.shape[0] - micro, length), jnp.int32)
    sum1[...] = jnp.zeros(sum1.shape, f32)
    sum2[...] = jnp.zeros(sum2.shape, f32)

    @pl.when(jnp.logical_not(has_left))
    def _():
        labels[0] = jnp.full(labels.shape[1:], -1, jnp.int32)
        sext[:, 0:length, :] = jnp.zeros((micro, length, inner), bf16)
        gext[:, 0:length, :] = jnp.zeros((micro, length, inner), bf16)

    @pl.when(jnp.logical_not(has_right))
    def _():
        labels[1] = jnp.full(labels.shape[1:], -1, jnp.int32)
        sext[:, 2 * length :, :] = jnp.zeros((micro, length, inner), bf16)
        gext[:, 2 * length :, :] = jnp.zeros((micro, length, inner), bf16)

    def halo(ext, turn, i):
        return (
            (
                has_right,
                pltpu.make_async_remote_copy(
                    src_ref=ext.at[i, pl.ds(length, length)],
                    dst_ref=ext.at[i, pl.ds(0, length)],
                    send_sem=halo_send.at[0, i],
                    recv_sem=halo_recv.at[turn, 0, i],
                    device_id=right,
                    device_id_type=MESH,
                ),
            ),
            (
                has_left,
                pltpu.make_async_remote_copy(
                    src_ref=ext.at[i, pl.ds(length, length)],
                    dst_ref=ext.at[i, pl.ds(2 * length, length)],
                    send_sem=halo_send.at[1, i],
                    recv_sem=halo_recv.at[turn, 1, i],
                    device_id=left,
                    device_id_type=MESH,
                ),
            ),
        )

    def label_copies():
        return [
            (
                ok,
                pltpu.make_async_remote_copy(
                    src_ref=own_labels,
                    dst_ref=labels.at[way],
                    send_sem=label_send.at[way],
                    recv_sem=label_recv.at[way],
                    device_id=target,
                    device_id_type=MESH,
                ),
            )
            for way, (ok, target) in enumerate(((has_right, right), (has_left, left)))
        ]

    def start_all(copies):
        for ok, copy in copies:
            pl.when(ok)(copy.start)

    def wait_sent(copies):
        for ok, copy in copies:
            pl.when(ok)(copy.wait_send)

    def wait_got(copies):
        pl.when(has_left)(copies[0][1].wait_recv)
        pl.when(has_right)(copies[1][1].wait_recv)

    def first_half(i, chunks=slice(None)):
        chunk = length // 2
        for begin in (0, chunk)[chunks]:
            some = pl.ds(begin, chunk)
            mean, scale, normal = normalise(x[i, some, :].astype(f32))
            act, slope = gelu_and_slope(normal * n1g[...] + n1s[...])
            first[i, some, :] = act.astype(bf16)
            slope1[i, some, :] = slope.astype(bf16)
            stat1[0, i, some, :] = jnp.broadcast_to(mean, (chunk, 128))
            stat1[1, i, some, :] = jnp.broadcast_to(scale, (chunk, 128))

    def second_half(i, reduced):
        _, scale, normal = normalise(reduced)
        act, slope = gelu_and_slope(normal * n2g[...] + n2s[...])
        sext[i, pl.ds(length, length), :] = act.astype(bf16)
        slope2[i] = slope.astype(bf16)
        normal2[i] = normal.astype(bf16)
        scale2[i] = jnp.broadcast_to(scale, (length, 128))

    def repeat(count, body):
        if z.unroll:
            for i in range(count):
                body(i)
        else:
            lax.fori_loop(0, count, lambda i, carry: (body(i), carry)[1], 0)

    for name, job in jobs.items():
        used, lanes = z.lanes(name)[1], job.send.shape[-1]
        if used < lanes:
            job.send[..., used:] = jnp.zeros(job.send.shape[:-1] + (lanes - used,), bf16)
    first_chunks[0].wait()
    for copy in vector_loads[:2]:
        copy.wait()
    first_half(0, slice(0, 1))
    first_chunks[1].wait()
    first_half(0, slice(1, 2))
    for copy in vector_loads[2:]:
        copy.wait()
    weight_loads[0].wait()

    def head(i, carry):
        load_x(i + 1).wait()
        reduced = dot(first[i], wd[...]) + db[...]
        first_half(i + 1)
        second_half(i, reduced)

        @pl.when(i == 0)
        def _():
            weight_loads[4].wait()
            pl.semaphore_wait(barrier, z.seq + z.rows - 2)
            start_all(label_copies())

        start_all(halo(sext, 0, i))
        return carry

    lax.fori_loop(0, micro - 1, head, 0)

    def third_grad_at(i):
        row, column = split(i)
        if isinstance(i, int):
            return pl.ds(row * length, length), pl.ds(column * inner, inner)
        return (
            pl.ds(pl.multiple_of(row * length, 128), length),
            pl.ds(pl.multiple_of(column * inner, 128), inner),
        )

    weight_loads[1].wait()
    weight_loads[3].wait()
    reduced = dot(first[micro - 1], wd[...]) + db[...]
    for i in range(0, micro, 2):
        grads = dot_cols(c[i : i + 2].reshape(2 * length, width), wu[...])
        for j in range(2):
            product[third_grad_at(i + j)] = grads[j * length : (j + 1) * length]
            sum1[0] += fold(c[i + j].astype(f32))
    second_half(micro - 1, reduced)
    start_all(halo(sext, 0, micro - 1))

    weight_loads[2].wait()
    wait_got(label_copies())
    wait_got(halo(sext, 0, 0))
    spread = jnp.concatenate([labels[0], own_labels[...], labels[1]], axis=1).astype(f32).T
    for i in range(micro):
        column = spread[:, i : i + 1]
        centre = column[length : 2 * length]
        for n, k in enumerate(k for k in range(taps) if k != taps // 2):
            begin = length - z.margin + k * DILATION
            same = (column[begin : begin + length] == centre).astype(f32)
            masks[n, i] = jnp.broadcast_to(same, (length, 128)).astype(bf16)

    def tap_of(ext, i, k):
        begin = length - z.margin + k * DILATION
        block = ext[i, pl.ds(begin, length), :]
        if k == taps // 2:
            return block
        keep = masks[k if k < taps // 2 else k - 1, i]
        return block * jnp.concatenate([keep] * (inner // 128), axis=1)

    def taps_of(ext, i):
        found = []
        for k in range(taps):
            block = tap_of(ext, i, k)
            if k != taps // 2:
                n = k if k < taps // 2 else k - 1
                masked[n] = block
                block = masked[n]
            found.append(block)
        return jnp.concatenate(found, axis=1)

    def convolve(i):
        if z.unroll:
            conv = dot(taps_of(sext, i), wc[...].reshape(taps * inner, inner))
        else:
            conv = sum(dot(tap_of(sext, i, k), wc[k]) for k in range(taps))
        return (conv + cb[...]).astype(bf16)

    parts = [pl.ds(begin, length // 4) for begin in range(0, length, length // 4)]

    def middle(i, part):
        some = parts[part]
        mixed = held[some, :].astype(f32)
        _, scale, normal = normalise(mixed)
        act, slope = gelu_and_slope(normal * n3g[...] + n3s[...])
        third[i, some, :] = act.astype(bf16)
        row, column = third_grad_at(i)
        grad = product[pl.ds(row.start + some.start, some.size), column] * slope
        sum2[0] += fold(grad * normal)
        sum2[1] += fold(grad)
        mixed_grad = norm_back(grad * n3g[...], normal, scale).astype(bf16)
        gext[i, pl.ds(length + some.start, some.size), :] = mixed_grad
        sum2[2] += fold(mixed_grad.astype(f32))

    held[...] = convolve(0)

    def middle_step(i, carry):
        wait_got(halo(sext, 0, i + 1))
        conv = convolve(i + 1)
        for part in range(len(parts)):
            middle(i, part)
        held[...] = conv
        wait_sent(halo(sext, 0, i))
        start_all(halo(gext, 1, i))
        return carry

    lax.fori_loop(0, micro - 1, middle_step, 0)
    for part in range(len(parts)):
        middle(micro - 1, part)
    wait_sent(halo(sext, 0, micro - 1))
    start_all(halo(gext, 1, micro - 1))

    def finish(name):
        value = jobs[name].finish()
        for matrix, tap, group, lane in z.lanes(name)[0]:
            rows, columns = z.share[matrix]
            target = {"up": up_out, "conv": conv_out.at[tap], "down": down_turned}[matrix]
            count = min(16, rows - 16 * group)
            target[pl.ds(16 * group, count), :] = value[:count, lane : lane + columns]

    whole = lambda ref: ref[...].reshape(z.positions, ref.shape[-1])
    own = lambda ext: ext[:, length : 2 * length, :].reshape(z.positions, inner)

    def pack(matrix, tap, base, rows_over):
        share = z.share[matrix]
        over_rows, over_columns = (z.rows, z.seq) if rows_over == "rows" else (z.seq, z.rows)
        targets = [
            (job, group, lane)
            for name, job in jobs.items()
            for m, t, group, lane in z.lanes(name)[0]
            if (m, t) == (matrix, tap)
        ]

        def pack_rows(k):
            begin = k * share[0]
            if not isinstance(k, int):
                begin = pl.multiple_of(begin, 8)
            rows = product[pl.ds(begin, share[0]), base : base + over_columns * share[1]]
            for j in range(over_columns):
                piece = rows[:, j * share[1] : (j + 1) * share[1]]
                for job, group, lane in targets:
                    at = job.index(k, j) if rows_over == "rows" else job.index(j, k)
                    some = piece[16 * group : min(16 * group + 16, share[0])]
                    short = 16 - some.shape[0]
                    if short:
                        some = jnp.concatenate([some, jnp.zeros((short, share[1]), f32)], axis=0)
                    job.send[at + (slice(None), pl.ds(lane, share[1]))] = some.astype(bf16)

        repeat(over_rows, pack_rows)

    def conv_weight_grad(k):
        if k == taps // 2:
            source = own(sext)
        else:
            for i in range(micro):
                masked[i] = tap_of(sext, i, k)
            source = whole(masked)
        base = k % 2 * inner
        product[:, base : base + inner] = dot_rows(source, own(gext))
        pack("conv", k, base, "rows")

    product[...] = dot_rows(whole(third), whole(c))
    pack("up", 0, 0, "rows")
    conv_weight_grad(0)
    conv_weight_grad(1)
    start_reductions("up", 0, 1)
    steps("up")
    for k in range(2, taps):
        conv_weight_grad(k)
    start_reductions(*range(2, taps))
    steps("conv")

    def convolve_back(i):
        if z.unroll:
            weights = jnp.concatenate([wc[taps - 1 - k] for k in range(taps)], axis=1)
            grad = dot_cols(taps_of(gext, i), weights)
        else:
            grad = sum(dot_cols(tap_of(gext, i, k), wc[taps - 1 - k]) for k in range(taps))
        return grad.astype(bf16)

    def second_back(i, part):
        some = parts[part]
        grad = held[some, :].astype(f32) * slope2[i, some, :].astype(f32)
        normal = normal2[i, some, :].astype(f32)
        sum2[3] += fold(grad * normal)
        sum2[4] += fold(grad)
        scale = jnp.concatenate([scale2[i, some, :]] * (inner // 128), axis=1)
        reduced_grad = norm_back(grad * n2g[...], normal, scale).astype(bf16)
        sext[i, some, :] = reduced_grad
        sum2[5] += fold(reduced_grad.astype(f32))

    wait_got(halo(gext, 1, 0))
    held[...] = convolve_back(0)
    steps("back0")

    def conv_back_step(i, carry):
        wait_got(halo(gext, 1, i + 1))
        grad = convolve_back(i + 1)
        for part in range(len(parts)):
            second_back(i, part)
        held[...] = grad

        steps_in("back", micro - 1, i + 1)
        return carry

    lax.fori_loop(0, micro - 1, conv_back_step, 0)
    for part in range(len(parts)):
        second_back(micro - 1, part)
    steps("back3")

    half = width // 2

    group, mine = lax.div(me_s, SLICES) * SLICES, lax.rem(me_s, SLICES)

    def vector_copies(turn, stage):
        own, got, part, far, total = vector_refs[5 * turn : 5 * turn + 5]
        me, count = ((me_s, z.seq), (me_r, z.rows), (mine, SLICES))[stage]
        inbox = (got, far, total)[stage]
        sends = []
        for off in range(1, count):
            other = lax.rem(me + off, count)
            target = ((me_r, other), (other, me_s), (me_r, group + other))[stage]
            source = (own.at[lax.rem(other, SLICES)], part, total.at[mine])[stage]
            sends.append(
                functools.partial(
                    pltpu.make_async_remote_copy,
                    src_ref=source,
                    dst_ref=inbox.at[me],
                    send_sem=vec_send.at[turn, stage],
                    recv_sem=vec_recv.at[turn, stage],
                    device_id=target,
                    device_id_type=MESH,
                )
            )
        return sends, inbox.at[pl.ds(0, count - 1)]

    def vector_start(turn, stage):
        for copy in vector_copies(turn, stage)[0]:
            copy().start()

    def vector_wait(turn, stage, sem):
        some = vector_copies(turn, stage)[1]
        pltpu.make_async_copy(some, some, sem.at[turn, stage]).wait()

    def vector_sent(turn):
        for stage in range(3):
            vector_wait(turn, stage, vec_send)

    def vector_step(turn, stage):
        own, got, part, far, total = vector_refs[5 * turn : 5 * turn + 5]
        vector_wait(turn, stage - 1, vec_recv)
        if stage == 3:
            rows = own.shape[1]
            for k in range(SLICES):
                begin = (0, 8)[turn] + k * rows
                vec_out[begin : begin + rows, :] = total[k]
            vector_sent(turn)
            return
        me, count = ((me_s, z.seq), (me_r, z.rows))[stage - 1]
        inbox = (got, far)[stage - 1]
        inbox[me] = (own[mine], part[...])[stage - 1]
        value = inbox[0]
        for k in range(1, count):
            value = value + inbox[k]
        if stage == 1:
            part[...] = value
        else:
            total[mine] = value
        vector_start(turn, stage)

    def squeeze(value):
        return jnp.sum(value, axis=0, keepdims=True)

    early = [squeeze(sum1[0, :, h * half : (h + 1) * half]) for h in range(2)]
    early += [squeeze(sum2[k]) for k in range(6)]
    for k, row in enumerate(early):
        vector_refs[0][k // 2, k % 2 : k % 2 + 1, :] = row
    vector_start(0, 0)

    reduced_grads = sext[:, 0:length, :].reshape(z.positions, inner)
    product[...] = dot_rows(reduced_grads, whole(first))
    pack("down", 0, 0, "seq")
    start_reductions("down")
    steps("down")

    def first_back(i, carry):
        grads = dot_cols(sext[i, pl.ds(0, length), :], wd[...])
        chunk = min(128, length)
        for begin in range(0, length, chunk):
            some = pl.ds(begin, chunk)
            grad = grads[begin : begin + chunk] * slope1[i, some, :].astype(f32)
            mean = jnp.concatenate([stat1[0, i, some, :]] * (width // 128), axis=1)
            scale = jnp.concatenate([stat1[1, i, some, :]] * (width // 128), axis=1)
            normal = (x[i, some, :].astype(f32) - mean) * scale
            sum1[1] += fold(grad * normal)
            sum1[2] += fold(grad)
            part = norm_back(grad * n1g[...], normal, scale)
            c[i, some, :] = (c[i, some, :].astype(f32) + part).astype(bf16)

        steps_in("first", micro - 1, i)
        return carry

    lax.fori_loop(0, micro, first_back, 0)
    late = [squeeze(sum1[k, :, h * half : (h + 1) * half]) for k in (1, 2) for h in range(2)]
    for k, row in enumerate(late):
        vector_refs[5][k] = row
    vector_start(1, 0)
    steps("first3")

    def finish_output(i, carry):
        x[i] = (x[i].astype(f32) + dot(third[i], wu[...]) + ub[...]).astype(bf16)

        steps_in("output", micro - 1, i)
        return carry

    lax.fori_loop(0, micro, finish_output, 0)
    for i in range(micro):
        wait_sent(halo(gext, 1, i))
    wait_sent(label_copies())
    steps("end")
    down_out[...] = down_turned[...].T


def per_device(z, x, seg, c, n1g, n1s, wd, db, n2g, n2s, wc, cb, n3g, n3s, wu, ub):
    micro, length, width, inner, taps = z.micro, z.length, z.width, z.inner, z.taps
    rows = lambda last, kind: pltpu.VMEM((micro, length, last), kind)
    job_scratch = []
    n = sizes_of(z.rows, z.seq)
    for name, (order, _) in JOBS.items():
        block = z.block(name)
        lead = tuple(n[d] for d in "c" + order)
        job_scratch.append(pltpu.VMEM(lead + block, bf16))
        for stage in range(len(lead)):
            job_scratch.append(pltpu.VMEM((lead[stage] - 1,) + lead[stage + 1 :] + block, bf16))
        job_scratch.append(pltpu.SemaphoreType.DMA((max(lead) - 1,)))
        job_scratch.append(pltpu.SemaphoreType.DMA((sum(lead) - len(lead),)))
    scratch = [
        pltpu.VMEM((width, inner), bf16),
        pltpu.VMEM((taps, inner, inner), bf16),
        pltpu.VMEM((inner, width), bf16),
        rows(width, bf16),
        rows(width, bf16),
        pltpu.VMEM((2, micro, length, 128), f32),
        rows(inner, bf16),
        rows(128, f32),
        rows(inner, bf16),
        pltpu.VMEM((micro, 3 * length, inner), bf16),
        pltpu.VMEM((micro, 3 * length, inner), bf16),
        pltpu.VMEM((taps - 1, micro, length, 128), bf16),
        rows(inner, bf16),
        rows(inner, bf16),
        pltpu.VMEM((length, inner), bf16),
        pltpu.VMEM((inner, width), f32),
        pltpu.VMEM((8, length), jnp.int32),
        pltpu.VMEM((2, 8, length), jnp.int32),
        pltpu.VMEM(z.share["down"], f32),
        pltpu.VMEM((3, 8, width), f32),
        pltpu.VMEM((6, 8, inner), f32),
    ] + [
        pltpu.VMEM(lead + (rows_of, inner), f32)
        for rows_of in (2, 1)
        for lead in ((SLICES,), (z.seq,), (), (z.rows,), (SLICES,))
    ] + [
        pltpu.SemaphoreType.DMA((micro_loads(z) + 10,)),
        pltpu.SemaphoreType.DMA((2, micro)),
        pltpu.SemaphoreType.DMA((2, 2, micro)),
        pltpu.SemaphoreType.DMA((2,)),
        pltpu.SemaphoreType.DMA((2,)),
    ] + [
        pltpu.VMEM(v.shape, f32) for v in (n1g, n1s, db, n2g, n2s, cb, n3g, n3s, ub)
    ] + [
        pltpu.SemaphoreType.DMA((2, 3))
        for _ in range(2)
    ] + job_scratch
    out, ig, vectors, down, conv, up = pl.pallas_call(
        functools.partial(kernel, z),
        out_shape=(
            pltpu.VMEM(x.shape, bf16),
            pltpu.VMEM(x.shape, bf16),
            pltpu.VMEM((16, inner), f32),
            pltpu.VMEM(z.share["down"][::-1], f32),
            pltpu.VMEM((taps,) + z.share["conv"], f32),
            pltpu.VMEM(z.share["up"], f32),
        ),
        in_specs=[ANY] * 15,
        out_specs=(VMEM,) * 6,
        scratch_shapes=scratch,
        compiler_params=pltpu.CompilerParams(
            collective_id=0, has_side_effects=True, vmem_limit_bytes=58 << 20
        ),
    )(
        x, seg, c, n1g, n1s, wd, db, n2g, n2s, wc, cb, n3g, n3s, wu, ub,
    )
    vector = lambda n: jax.ShapeDtypeStruct((n,), f32)
    out, ig, down, conv, up, *vectors = pl.pallas_call(
        write_out,
        out_shape=(
            jax.ShapeDtypeStruct(x.shape, bf16),
            jax.ShapeDtypeStruct(x.shape, bf16),
            jax.ShapeDtypeStruct(z.share["down"][::-1], f32),
            jax.ShapeDtypeStruct((taps,) + z.share["conv"], f32),
            jax.ShapeDtypeStruct(z.share["up"], f32),
        )
        + tuple(vector(width if first + 1 < last else inner) for first, last in VECTORS),
        in_specs=[VMEM] * 6,
        out_specs=(ANY,) * (5 + len(VECTORS)),
        scratch_shapes=[pltpu.VMEM((width if first + 1 < last else inner,), f32) for first, last in VECTORS]
        + [pltpu.SemaphoreType.DMA((5 + len(VECTORS),))],
        compiler_params=pltpu.CompilerParams(vmem_limit_bytes=2 << 20),
    )(*(pltpu.with_memory_space_constraint(v, pltpu.VMEM) for v in (out, ig, vectors, down, conv, up)))
    ub, n3g, n3s, cb, n2g, n2s, db, n1g, n1s = vectors
    return out, ig, n1g, n1s, down, db, n2g, n2s, conv, cb, n3g, n3s, up, ub


VECTORS = ((0, 2), (2, 3), (3, 4), (4, 5), (5, 6), (6, 7), (7, 8), (8, 10), (10, 12))


def write_out(out, ig, vectors, down, conv, up, *rest):
    count = len(VECTORS)
    targets, rows, sem = rest[: 5 + count], rest[5 + count : -1], rest[-1]
    width = vectors.shape[1]
    sources = (out, ig, down, conv, up) + rows
    copies = [
        pltpu.make_async_copy(source, target, sem.at[k])
        for k, (source, target) in enumerate(zip(sources, targets))
    ]
    for copy in copies[:5]:
        copy.start()
    for row, (begin, end) in zip(rows, VECTORS):
        for k in range(begin, end):
            row[pl.ds((k - begin) * width, width)] = vectors[k, :]
    for copy in copies[5:]:
        copy.start()
    for copy in copies:
        copy.wait()


def solution(mesh):
    def step(*args):
        micro, length, width = args[0].shape
        taps, inner, _ = args[9].shape
        z = Sizes(mesh.shape["rows"], mesh.shape["seq"], micro, length, width, inner, taps)
        return per_device(z, *args)

    rows = P("rows", "seq", None)
    matrix = P("rows", "seq")
    return jax.shard_map(
        step,
        mesh=mesh,
        in_specs=(rows, matrix, rows) + (P(),) * 12,
        out_specs=(rows, rows, P(), P(), matrix, P(), P(), P(), P(None, "rows", "seq"))
        + (P(),) * 3
        + (matrix, P()),
        check_vma=False,
    )
```
